32 devices in a mesh: groups: 2 (over y), tm: 4 (over z), space: 4 (over x, core).
Axes of the slice: x: 2, y: 2, z: 4, core: 2. Of those that a mesh axis runs over, the one named last changes fastest.
Arguments:
- frames_in: bfloat16 [64, 112896], P(('groups', 'tm'), 'space'), parts along dimension 0, may hold values from -6 to 6
- arrive_len: int32 [8], P('groups'), parts along dimension 0, may hold values from 1 to 8, 16 in all
- clip_len: int32 [8], P('groups'), parts along dimension 0, may hold values from 1 to 8, 16 in all
- tile_pick: int32 [392, 196], P('groups'), parts along dimension 0, may hold values from 0 to 1, as said below
- norm_gain: float32 [576], replicated, may hold values from 0.5 to 1.5
- in_weight: bfloat16 [2, 576, 1152], replicated, may hold values from -0.25 to 0.25
- proj_weight: bfloat16 [4, 1152, 68], P(None, 'space'), may hold values from -0.1875 to 0.1875
- dt_weight: bfloat16 [4, 36, 1152], P(None, None, 'space'), may hold values from -1 to 1
- dt_bias: float32 [4, 1152], P(None, 'space'), may hold values from -4 to -1
- decay_rate: float32 [4, 1152, 16], P(None, 'space'), may hold values from 0.05 to 4
- skip_gain: float32 [4, 1152], P(None, 'space'), may hold values from 0.5 to 1.5
- out_weight: bfloat16 [1152, 576], P('space'), may hold values from -0.1875 to 0.1875
Outputs:
- mixed: bfloat16 [196, 18432], P('tm', ('groups', 'space')), parts along dimension 1
The draws below stay inside these ranges and needn't reach their ends.
There are 2 independent parts, one for each index of `groups`. The reference program is written for one: setup_inputs(seed, part) draws one part's arguments, and reference() takes and returns one part's arrays. A program takes and returns all parts, laid end to end along the dimension named above; an argument that names none is the same for every part. Nothing has to cross between parts.
Inputs may be any that keep to these rules, and one draw needn't show every extreme that they name: Device j of tm holds in its first arrive_len[j] slots the blocks of the packed sequence that follow those of devices before it; its other slots are padding. `clip_len`: the clips cover the 16 frames end to end. `tile_pick`: each patch has exactly one 1 in its row; each column holds at most one 1; the 49 columns of each device of tm are used from its first one on, 49 or 48 of them.
All inputs are finite; a program needn't handle non-finite values.
Results may differ from the reference program's by a relative error of at most 0.015.
Values may be sent and summed in bfloat16 or wider, within the bound.
A program may use at most 64 MiB of HBM per device.

```python
import math
import jax
import jax.numpy as jnp
import numpy as np
from jax import lax

D = 576
E = 1152
STATE = 16
DT_RANK = 36
PATCHES = 196
BF = 1
OWN_BLK = 4
IN_BLK = 8
FRAMES = 16
MAXCLIP = 8
PT = 49
TILES = 196
N_TM = 4
N_SPACE = 4


def draw_tile_pick(key, part):
    key = jax.random.fold_in(key, 7)
    first_key, second_key = jax.random.split(key)
    patch_order = jax.random.permutation(first_key, PATCHES)
    owner_order = jax.random.permutation(second_key, N_TM)
    position = jnp.arange(PATCHES, dtype=jnp.int32)
    column = owner_order[position % N_TM] * PT + position // N_TM
    return jnp.zeros((PATCHES, TILES), jnp.int32).at[patch_order, column].set(1)


def level_of(key, dims, pieces, smallest, high):
    gain = 1.0
    for dim, parts in pieces:
        draws = jax.random.uniform(jax.random.fold_in(jax.random.fold_in(key, 6), dim), (parts,), jnp.float32, smallest / len(pieces), high / len(pieces))
        gain = gain * jnp.repeat(jnp.exp(draws), dims[dim] // parts).reshape((-1,) + (1,) * (len(dims) - 1 - dim))
    return gain


def profile(amount, total, most, slope):
    weights = [(1 << 20) // math.isqrt(rank ** slope) + 1 for rank in range(2, amount + 1)]
    surplus, holding = total - most - (amount - 1), [1] * (amount - 1)
    while surplus > 0:
        movable = [i for i in range(amount - 1) if holding[i] < most]
        pool, budget = sum([weights[i] for i in movable]), surplus
        for i in movable:
            addition = min(most - holding[i], max(1, budget * weights[i] // pool), surplus)
            holding[i] = holding[i] + addition
            surplus = surplus - addition
    return np.array([most] + holding)


def uneven(key, amount, total, reach, skew):
    if amount == 2:
        one = jax.random.randint(key, (), max(1, total - reach), min(reach, total - 1) + 1)
        return jnp.stack([one, total - one])
    lengths = jnp.asarray(profile(amount, total, reach, skew), jnp.int32)
    pairs = (amount - 1) // 2
    giver, taker = lengths[1:1 + 2 * pairs:2], lengths[2:2 + 2 * pairs:2]
    margin = jnp.minimum(giver - 1, reach - taker)
    shifted = jax.random.randint(jax.random.fold_in(key, 1), (pairs,), 0, 1 << 20) % (margin + 1)
    lengths = lengths.at[1:1 + 2 * pairs:2].set(giver - shifted).at[2:2 + 2 * pairs:2].set(taker + shifted)
    return lengths[jax.random.permutation(jax.random.fold_in(key, 2), amount)]


def noise(key, extent, deviation, bound, pieces=(), held_as=jnp.bfloat16):
    entries = jax.random.normal(key, extent, jnp.float32) * deviation
    if len(pieces) > 0:
        entries = level_of(key, extent, pieces, -0.22, 0.18) * entries
    return jnp.clip(entries, min=-bound, max=bound).astype(held_as)


def setup_inputs(seed: int = 0, part: int = 0) -> dict:
    keys = jax.random.split(jax.random.key(seed), 13)
    part_splits = jax.random.split(jax.random.fold_in(keys[12], part), 13)
    return {
        "frames_in": noise(part_splits[0], (N_TM * IN_BLK, BF * PATCHES * D), 1.0, 6.0, ((0, 4), (1, 4))),
        "arrive_len": uneven(part_splits[1], N_TM, N_TM * OWN_BLK, IN_BLK, 2).astype(jnp.int32),
        "clip_len": uneven(part_splits[2], N_TM, FRAMES, MAXCLIP, 2).astype(jnp.int32),
        "tile_pick": draw_tile_pick(jax.random.fold_in(jax.random.fold_in(keys[12], part), 71), part),
        "norm_gain": jnp.clip(1.0 + 0.1 * jax.random.normal(keys[4], (D,), jnp.float32), 0.5, 1.5),
        "in_weight": noise(keys[5], (2, D, E), D ** -0.5, 0.25),
        "proj_weight": noise(keys[6], (4, E, DT_RANK + 2 * STATE), E ** -0.5, 0.1875, ((1, 4),)),
        "dt_weight": noise(keys[7], (4, DT_RANK, E), DT_RANK ** -0.5, 1.0, ((2, 4),)),
        "dt_bias": jnp.clip(-4.0 + 3.0 * jax.random.uniform(keys[8], (4, E), jnp.float32) ** level_of(keys[8], (4, E), ((1, 4),), -0.2, 0.2), -4.0, -1.0),
        "decay_rate": jnp.clip(jnp.exp(math.log(4.0) - 4.3820266 * jax.random.uniform(keys[9], (4, E, STATE), jnp.float32) ** level_of(keys[9], (4, E, STATE), ((1, 4),), -0.2, 0.2)), 0.05, 4.0),
        "skip_gain": jnp.clip(0.5 + 1.0 * jax.random.uniform(keys[10], (4, E), jnp.float32) ** level_of(keys[10], (4, E), ((1, 4),), -0.2, 0.2), 0.5, 1.5),
        "out_weight": noise(keys[11], (E, D), E ** -0.5, 0.1875, ((0, 4),)),
    }


EPSILON = 1e-05

def directed_scan(values, stats_set, dt_matrix, dt_offset, decay_rates, skip_vec, keep_flags, reverse):
    low_rank = dt_matrix.shape[0]
    state_width = decay_rates.shape[1]

    def advance(carried, inputs):
        value_now, stat_now, keep_now = inputs
        value_float = value_now.astype(jnp.float32)
        delta = jax.nn.softplus(jnp.dot(stat_now[:, :low_rank], dt_matrix, preferred_element_type=jnp.float32) + dt_offset)
        in_gate = stat_now[:, low_rank:low_rank + state_width].astype(jnp.float32)
        out_gate = stat_now[:, low_rank + state_width:].astype(jnp.float32)
        carried = keep_now * jnp.exp(-delta[:, :, None] * decay_rates) * carried + (delta * value_float)[:, :, None] * in_gate[:, None, :]
        return (carried, lax.optimization_barrier(jnp.sum(carried * out_gate[:, None, :], axis=2)) + skip_vec * value_float)
    initial = jnp.zeros((values.shape[1], values.shape[2], state_width), jnp.float32)
    _, outputs = lax.scan(advance, initial, (values, stats_set, keep_flags), reverse=reverse)
    return outputs

def reference(frames_in, arrive_len, clip_len, tile_pick, norm_gain, in_weight, proj_weight, dt_weight, dt_bias, decay_rate, skip_gain, out_weight):
    offsets = jnp.cumsum(arrive_len) - arrive_len
    slot_ids = jnp.arange(N_TM * IN_BLK, dtype=jnp.int32)
    sender = slot_ids // IN_BLK
    within = slot_ids % IN_BLK
    target = jnp.where(within < arrive_len[sender], offsets[sender] + within, N_TM * OWN_BLK).astype(jnp.int32)
    source = jnp.zeros((N_TM * OWN_BLK,), jnp.int32).at[target].set(slot_ids, mode='drop')
    blocks = frames_in.reshape(N_TM * IN_BLK, BF, PATCHES, D)
    frames = jnp.take(blocks, source, axis=0).reshape(FRAMES, PATCHES, D)
    row_float = frames.astype(jnp.float32)
    inv_scale = lax.rsqrt(lax.optimization_barrier(jnp.mean(row_float * row_float, axis=2, keepdims=True)) + EPSILON)
    normed = (row_float * inv_scale * norm_gain).astype(jnp.bfloat16)
    flat_rows = normed.reshape(FRAMES * PATCHES, D)
    inner_act = jax.nn.silu(jnp.dot(flat_rows, in_weight[0], preferred_element_type=jnp.float32)).astype(jnp.bfloat16)
    gate_value = jnp.dot(flat_rows, in_weight[1], preferred_element_type=jnp.float32).astype(jnp.bfloat16)
    stats = [jnp.dot(inner_act, proj_weight[set_index], preferred_element_type=jnp.float32).astype(jnp.bfloat16).reshape(FRAMES, PATCHES, -1) for set_index in range(4)]
    inner_grid = inner_act.reshape(FRAMES, PATCHES, E)
    by_patch = jnp.swapaxes(inner_grid, 0, 1)
    keep_all = jnp.ones((PATCHES,), jnp.float32)
    spatial_sum = jnp.zeros((PATCHES, FRAMES, E), jnp.float32)
    for set_index, backward in ((0, False), (1, True)):
        spatial_sum = spatial_sum + directed_scan(by_patch, jnp.swapaxes(stats[set_index], 0, 1), dt_weight[set_index], dt_bias[set_index], decay_rate[set_index], skip_gain[set_index], keep_all, backward)
    spatial = jnp.swapaxes(spatial_sum, 0, 1).astype(jnp.bfloat16)
    clip_start = jnp.cumsum(clip_len) - clip_len
    frame_ids = jnp.arange(FRAMES, dtype=jnp.int32)
    first_keep = 1.0 - jnp.any(frame_ids[:, None] == clip_start[None, :], axis=1).astype(jnp.float32)
    last_keep = 1.0 - jnp.any(frame_ids[:, None] == (clip_start + clip_len - 1)[None, :], axis=1).astype(jnp.float32)
    temporal = directed_scan(inner_grid, stats[2], dt_weight[2], dt_bias[2], decay_rate[2], skip_gain[2], first_keep, False)
    temporal = temporal + directed_scan(inner_grid, stats[3], dt_weight[3], dt_bias[3], decay_rate[3], skip_gain[3], last_keep, True)
    gated = ((spatial.astype(jnp.float32) + temporal) * jax.nn.silu(gate_value.reshape(FRAMES, PATCHES, E).astype(jnp.float32))).astype(jnp.bfloat16)
    gated_flat = gated.reshape(FRAMES * PATCHES, E)
    group_width = E // N_SPACE
    summed = jnp.zeros((FRAMES * PATCHES, D), jnp.float32)
    for group_index in range(N_SPACE):
        low_edge = group_index * group_width
        group_term = jnp.dot(gated_flat[:, low_edge:low_edge + group_width], out_weight[low_edge:low_edge + group_width], preferred_element_type=jnp.float32)
        summed = summed + lax.optimization_barrier(group_term.astype(jnp.bfloat16)).astype(jnp.float32)
    result = summed.astype(jnp.bfloat16).reshape(FRAMES, PATCHES, D)
    pick_source = lax.optimization_barrier(jnp.sum(tile_pick * jnp.arange(PATCHES, dtype=jnp.int32)[:, None], axis=0)).astype(jnp.int32)
    pick_live = lax.optimization_barrier(jnp.sum(tile_pick, axis=0)) > 0
    picked = jnp.take(result, pick_source, axis=1)
    picked = jnp.where(pick_live[None, :, None], picked, jnp.zeros_like(picked))
    return jnp.swapaxes(picked, 0, 1).reshape(TILES, FRAMES * D)
```

```python
import functools

import jax
import jax.numpy as jnp
import numpy as np
from jax import lax
from jax.experimental import pallas as pl
from jax.experimental.pallas import tpu as pltpu
from jax.sharding import PartitionSpec as P

PATCHES = 196
OWN_BLK = 4
IN_BLK = 8
ROWS = 4
STATE = 16
RANK = 36
HALF = 2 * (RANK + 2 * STATE)
EPSILON = 1e-05
LOG2E = 1.4426950408889634
CLOSED = 1e4
F32 = jnp.float32
BF16 = jnp.bfloat16


def chunks_of(part):
    assert 0 < part % 128 <= 32
    return tuple((512 * i, 512) for i in range(part // 128)) + ((512 * (part // 128), 128),)


def lanes_of(part):
    return 512 * (part // 128) + 128


def constants():
    perm = np.zeros((512, 512), np.float32)
    for r in range(ROWS):
        for ch in range(128):
            perm[r * 128 + ch, (ch // 32) * 128 + r * 32 + ch % 32] = 1
    spread = np.zeros((ROWS * STATE, STATE * 128), np.float32)
    for r in range(ROWS):
        for s in range(STATE):
            spread[r * STATE + s, s * 128 + r * 32 : s * 128 + r * 32 + 32] = 1
    return perm, spread


def widening(part):
    widen = np.zeros((part, lanes_of(part)), np.float32)
    for ch in range(part):
        for r in range(ROWS):
            widen[ch, (ch // 32) * 128 + r * 32 + ch % 32] = 1
    return widen


PERM, SPREAD = constants()


def dot(a, b):
    return jnp.dot(a, b, preferred_element_type=F32)


def pack_rows(wide, tail, perm_ref, chunk, size):
    wide = wide if size == 512 else None
    if wide is not None:
        return dot(jnp.concatenate([wide(r, chunk) for r in range(ROWS)], axis=1), perm_ref[...])
    total = 0.0
    for r in range(ROWS):
        piece = tail(r)
        total = total + dot(piece, perm_ref[128 * r : 128 * r + piece.shape[1], 0:128])
    return total


def store_tiles(ref, k, start, block):
    rows = ref.shape[1]
    flat = ref.reshape(2, rows * STATE, 128)
    for t in range(block.shape[1] // 128):
        flat[k, pl.ds(start // 128 + t, rows, stride=STATE), :] = block[:, 128 * t : 128 * t + 128]


def load_tiles(ref, k, start, size):
    rows = ref.shape[1]
    flat = ref.reshape(2, rows * STATE, 128)
    parts = [flat[k, pl.ds(start // 128 + t, rows, stride=STATE), :] for t in range(size // 128)]
    return jnp.concatenate(parts, axis=1)


def prepare(part, values, stats_ref, closed, weights, scratch):
    perm_ref, spread_ref, dt_ref, bias_ref = weights
    u_ref, d_ref, x_ref, b_ref, c_ref = scratch
    wide, tail = values
    stats = [stats_ref[r].astype(F32) for r in range(ROWS)]
    for k in range(2):
        low = jnp.concatenate([s[:, RANK * k : RANK * k + RANK] for s in stats], axis=1).astype(BF16)
        for chunk, (start, size) in enumerate(chunks_of(part)):
            cols = slice(start, start + size)
            if k == 0:
                u_ref[:, cols] = pack_rows(wide, tail, perm_ref, chunk, size)
            delta = dot(low, dt_ref[k, :, cols]) + bias_ref[k, :, cols]
            delta = jnp.maximum(delta, 0.0) + jnp.log1p(jnp.exp(-jnp.abs(delta)))
            store_tiles(x_ref, k, start, delta * u_ref[:, cols])
            if closed is not None:
                delta = jnp.where(closed[k] > 0.0, CLOSED, delta)
            store_tiles(d_ref, k, start, delta)
        for which, out_ref in ((0, b_ref), (1, c_ref)):
            at = 2 * RANK + STATE * (2 * k + which)
            picked = jnp.concatenate([s[:, at : at + STATE] for s in stats], axis=1).astype(BF16)
            for q in range(4):
                block = dot(picked, spread_ref[:, 512 * q : 512 * q + 512])
                store_tiles(out_ref, k, 512 * q, block)


def scan(k, steps, unroll, row_of, scratch, rate_ref, y_ref):
    u_ref, d_ref, x_ref, b_ref, c_ref = scratch
    tiles = u_ref.shape[1] // 128

    def step(i, state):
        row = row_of(i)
        b_now = b_ref[k, row]
        c_now = c_ref[k, row]
        after = []
        for t in range(tiles):
            cols = slice(128 * t, 128 * t + 128)
            d_now = jnp.broadcast_to(d_ref[k, row, t : t + 1, :], (STATE, 128))
            x_now = jnp.broadcast_to(x_ref[k, row, t : t + 1, :], (STATE, 128))
            h = jnp.exp2(d_now * rate_ref[k, :, cols]) * state[t] + x_now * b_now
            y_ref[k, row, t : t + 1, :] = jnp.sum(h * c_now, axis=0, keepdims=True)
            after.append(h)
        return tuple(after)

    start = tuple(jnp.zeros((STATE, 128), F32) for _ in range(tiles))
    lax.fori_loop(0, steps, step, start, unroll=unroll)


def first_kernel(x_ref, w_ref, gain_ref, proj_ref, pick_ref, inner_ref, stats_ref, tiles_ref):
    x = x_ref[0].astype(F32)
    scale = lax.rsqrt(jnp.mean(x * x, axis=1, keepdims=True) + EPSILON)
    normed = (x * scale * gain_ref[...]).astype(BF16)
    both = dot(normed, w_ref[...])

    def silu(v):
        return (v * jax.nn.sigmoid(v)).astype(BF16)

    part = inner_ref.shape[2]
    cut = part // 128 * 128
    end = part + cut
    main, last = silu(both[:, :cut]), silu(both[:, 2 * cut : end])
    inner_ref[0, :, :cut] = main
    inner_ref[0, :, cut:] = last
    stats_ref[0] = (dot(main, proj_ref[:cut, :]) + dot(last, proj_ref[cut:, :])).astype(BF16)
    pick = pick_ref[...]
    tiles_ref[0, :, :cut] = dot(pick, main).astype(BF16)
    tiles_ref[0, :, cut : 2 * cut] = dot(pick, both[:, cut : 2 * cut].astype(BF16)).astype(BF16)
    tiles_ref[0, :, 2 * cut : end] = dot(pick, last).astype(BF16)
    tiles_ref[0, :, end:] = dot(pick, both[:, end:].astype(BF16)).astype(BF16)


def spatial_kernel(
    inner_ref, stats_ref, pick_ref, perm_ref, inverse_ref, spread_ref, dt_ref, bias_ref, rate_ref,
    skip_ref, out_ref, u_ref, d_ref, x_ref, b_ref, c_ref, y_ref
):
    scratch = (u_ref, d_ref, x_ref, b_ref, c_ref)
    length, part = u_ref.shape[0], inner_ref.shape[2]
    cut = part // 128 * 128
    tail = part - cut
    values = (
        lambda r, c: inner_ref[r, :, 128 * c : 128 * c + 128],
        lambda r: inner_ref[r, :, cut:],
    )
    prepare(part, values, stats_ref, None, (perm_ref, spread_ref, dt_ref, bias_ref), scratch)
    scan(0, length, 4, lambda i: i, scratch, rate_ref, y_ref)
    scan(1, length, 4, lambda i: length - 1 - i, scratch, rate_ref, y_ref)
    pick = pick_ref[...]
    for start, size in chunks_of(part):
        cols = slice(start, start + size)
        total = load_tiles(y_ref, 0, start, size) + load_tiles(y_ref, 1, start, size)
        total = total + skip_ref[:, cols] * u_ref[:, cols]
        total = dot(pick, total.astype(BF16)).astype(BF16)
        if size == 512:
            back = dot(total, inverse_ref[...]).astype(BF16)
            for r in range(ROWS):
                at = start // 4
                out_ref[r, :, at : at + 128] = back[:, 128 * r : 128 * r + 128]
        else:
            for r in range(ROWS):
                back = dot(total, inverse_ref[0:128, 128 * r : 128 * r + tail])
                out_ref[r, :, cut:] = back.astype(BF16)


def temporal_kernel(
    frames, groups, both_ref, spatial_ref, stats_ref, closed_ref, perm_ref, inverse_ref, spread_ref,
    dt_ref, bias_ref, rate_ref, skip_ref, w_ref, out_ref, u_ref, d_ref, x_ref, b_ref, c_ref, y_ref
):
    scratch = (u_ref, d_ref, x_ref, b_ref, c_ref)
    owners, part = frames // OWN_BLK, spatial_ref.shape[2]
    cut = part // 128 * 128
    tail = part - cut
    values = (
        lambda r, c: both_ref[r, :, 128 * c : 128 * c + 128],
        lambda r: both_ref[r, :, 2 * cut : 2 * cut + tail],
    )
    closed = (closed_ref[:, 0:1], closed_ref[:, 1:2])
    prepare(part, values, stats_ref, closed, (perm_ref, spread_ref, dt_ref, bias_ref), scratch)

    def row_at(i, backward):
        group, frame = i // frames, i % frames
        if backward:
            frame = frames - 1 - frame
        return ((frame % owners) * OWN_BLK + frame // owners) * groups + group

    steps = frames * groups
    scan(0, steps, 4, lambda i: row_at(i, False), scratch, rate_ref, y_ref)
    scan(1, steps, 4, lambda i: row_at(i, True), scratch, rate_ref, y_ref)
    gate = (
        lambda r, c: both_ref[r, :, cut + 128 * c : cut + 128 * c + 128],
        lambda r: both_ref[r, :, 2 * cut + tail :],
    )
    spatial = (
        lambda r, c: spatial_ref[r, :, 128 * c : 128 * c + 128],
        lambda r: spatial_ref[r, :, cut:],
    )
    backs = []
    for chunk, (start, size) in enumerate(chunks_of(part)):
        cols = slice(start, start + size)
        total = load_tiles(y_ref, 0, start, size) + load_tiles(y_ref, 1, start, size)
        total = total + skip_ref[:, cols] * u_ref[:, cols]
        total = total + pack_rows(*spatial, perm_ref, chunk, size)
        g = pack_rows(*gate, perm_ref, chunk, size)
        total = (total * (g * jax.nn.sigmoid(g))).astype(BF16)
        if size == 512:
            backs.append(dot(total, inverse_ref[...]).astype(BF16))
        else:
            backs.append(total)
    for r in range(ROWS):
        lanes = slice(128 * r, 128 * r + 128)
        last = dot(backs[-1], inverse_ref[0:128, 128 * r : 128 * r + tail]).astype(BF16)
        term = dot(last, w_ref[cut:, :])
        for c in range(cut // 128):
            term = term + dot(backs[c][:, lanes], w_ref[128 * c : 128 * c + 128, :])
        out_ref[r] = term.astype(BF16)


def scan_scratch(rows, part):
    return [pltpu.VMEM((rows, lanes_of(part)), F32)] + [pltpu.VMEM((2, rows, STATE, 128), F32)] * 5


def call(kernel, out_shape, scratch, flops, *operands):
    return pl.pallas_call(
        kernel,
        out_shape=out_shape,
        in_specs=[pl.BlockSpec(memory_space=pltpu.VMEM)] * len(operands),
        out_specs=pl.BlockSpec(memory_space=pltpu.VMEM),
        scratch_shapes=scratch,
        compiler_params=pltpu.CompilerParams(vmem_limit_bytes=56 * 1024 * 1024),
        cost_estimate=pl.CostEstimate(flops=flops, bytes_accessed=8_000_000, transcendentals=7_000_000),
    )(*operands)


def body(
    frames_in, arrive_len, clip_len, tile_pick, norm_gain, in_weight, proj_weight, dt_weight, dt_bias,
    decay_rate, skip_gain, out_weight
):
    owners = lax.axis_size("tm")
    my_owner = lax.axis_index("tm")
    space_index = lax.axis_index("space")
    patches = PATCHES
    width = in_weight.shape[1]
    part = out_weight.shape[0]
    cut = part // 128 * 128
    frames_total = owners * OWN_BLK
    per_owner = tile_pick.shape[1] // owners
    groups = -(-per_owner // ROWS)
    slots = ROWS * groups

    weight = lax.dynamic_slice_in_dim(in_weight, space_index * part, part, 2)
    weight = jnp.concatenate(
        [weight[0, :, :cut], weight[1, :, :cut], weight[0, :, cut:], weight[1, :, cut:]], axis=1
    )
    widen = jnp.asarray(widening(part))
    exact = functools.partial(
        jnp.einsum, precision=lax.Precision.HIGHEST, preferred_element_type=F32
    )
    rate = exact("kcs,cn->ksn", decay_rate, widen) * -LOG2E
    bias = exact("kc,cn->kn", dt_bias, widen)[:, None, :]
    skip = exact("kc,cn->kn", skip_gain, widen)
    dt_wide = jnp.einsum(
        "kic,cn->kin", dt_weight, widen.astype(BF16), preferred_element_type=F32
    ).astype(BF16)
    lane_row = (jnp.arange(lanes_of(part), dtype=jnp.int32) % 128) // 32
    same = (lane_row[None, :] == jnp.arange(ROWS, dtype=jnp.int32)[:, None])[None, :, None, :]
    dt_wide = jnp.where(same, dt_wide[:, None], jnp.zeros((), BF16)).reshape(4, ROWS * RANK, lanes_of(part))
    pieces = []
    for half in (0, 2):
        pieces += [proj_weight[half, :, :RANK], proj_weight[half + 1, :, :RANK]]
        pieces += [proj_weight[half, :, RANK:], proj_weight[half + 1, :, RANK:]]
    proj = jnp.concatenate(pieces, axis=1)
    pick = tile_pick.astype(BF16).T.reshape(owners, per_owner, patches)
    pick = jnp.pad(pick, ((0, 0), (0, slots - per_owner), (0, 0))).reshape(owners * slots, patches)
    perm, inverse = jnp.asarray(PERM, BF16), jnp.asarray(PERM.T, BF16)
    spread = jnp.asarray(SPREAD, BF16)

    capacity = (IN_BLK + owners - 1) // owners
    offsets = jnp.cumsum(arrive_len) - arrive_len
    lane_index = jnp.arange(capacity, dtype=jnp.int32)[None, :]
    target_ids = jnp.arange(owners, dtype=jnp.int32)[:, None]
    slot_index = (target_ids - offsets[my_owner]) % owners + lane_index * owners
    packed = jnp.take(frames_in, jnp.minimum(slot_index, IN_BLK - 1).reshape(-1), axis=0)
    arrived = lax.all_to_all(packed, "tm", split_axis=0, concat_axis=0, tiled=True)
    wanted = jnp.arange(OWN_BLK, dtype=jnp.int32) * owners + my_owner
    sender = jnp.sum((offsets[None, :] <= wanted[:, None]).astype(jnp.int32), axis=1) - 1
    lane_of = (wanted - offsets[sender]) // owners
    owned = jnp.take(arrived, sender * capacity + lane_of, axis=0)
    full = lax.all_gather(owned, "space", axis=1, tiled=True).reshape(OWN_BLK, patches, width)

    inner, stats, tiles = pl.pallas_call(
        first_kernel,
        grid=(OWN_BLK,),
        out_shape=(
            jax.ShapeDtypeStruct((OWN_BLK, patches, part), BF16),
            jax.ShapeDtypeStruct((OWN_BLK, patches, 2 * HALF), BF16),
            jax.ShapeDtypeStruct((OWN_BLK, owners * slots, 2 * part), BF16),
        ),
        in_specs=[
            pl.BlockSpec((1, patches, width), lambda i: (i, 0, 0)),
            pl.BlockSpec((width, 2 * part), lambda i: (0, 0)),
            pl.BlockSpec((1, width), lambda i: (0, 0)),
            pl.BlockSpec((part, 2 * HALF), lambda i: (0, 0)),
            pl.BlockSpec((owners * slots, patches), lambda i: (0, 0)),
        ],
        out_specs=(
            pl.BlockSpec((1, patches, part), lambda i: (i, 0, 0)),
            pl.BlockSpec((1, patches, 2 * HALF), lambda i: (i, 0, 0)),
            pl.BlockSpec((1, owners * slots, 2 * part), lambda i: (i, 0, 0)),
        ),
        compiler_params=pltpu.CompilerParams(vmem_limit_bytes=32 * 1024 * 1024),
        cost_estimate=pl.CostEstimate(flops=900_000_000, bytes_accessed=4_000_000, transcendentals=250_000),
    )(full, weight, norm_gain[None, :], proj, pick)
    stats = lax.psum(stats, "space")

    def to_owner(array):
        moved = lax.all_to_all(array, "tm", split_axis=1, concat_axis=0, tiled=True)
        moved = moved.reshape(frames_total, ROWS, groups, array.shape[-1])
        return jnp.swapaxes(moved, 0, 1).reshape(ROWS, frames_total * groups, array.shape[-1])

    time_both = to_owner(tiles)
    late = jnp.einsum("sp,lpc->lsc", pick, stats[:, :, HALF:], preferred_element_type=F32)
    time_stats = to_owner(late.astype(BF16))
    spatial = call(
        spatial_kernel,
        jax.ShapeDtypeStruct((OWN_BLK, owners * slots, part), BF16),
        scan_scratch(patches, part),
        600_000_000,
        inner, stats[:, :, :HALF], pick, perm, inverse, spread, dt_wide[:2], bias[:2], rate[:2],
        (skip[0] + skip[1])[None, :],
    )
    time_spatial = to_owner(spatial)

    clip_start = jnp.cumsum(clip_len) - clip_len
    row_frame = jnp.arange(frames_total, dtype=jnp.int32)
    row_frame = (row_frame % OWN_BLK) * owners + row_frame // OWN_BLK
    opens = jnp.any(row_frame[:, None] == clip_start[None, :], axis=1) | (row_frame == 0)
    closes = jnp.any(row_frame[:, None] == (clip_start + clip_len - 1)[None, :], axis=1)
    closes = closes | (row_frame == frames_total - 1)
    closed = jnp.stack([opens, closes], axis=1).astype(F32)
    closed = jnp.repeat(closed, groups, axis=0)
    rows = frames_total * groups
    term = call(
        functools.partial(temporal_kernel, frames_total, groups),
        jax.ShapeDtypeStruct((ROWS, rows, width), BF16),
        scan_scratch(rows, part),
        600_000_000,
        time_both, time_spatial, time_stats, closed, perm, inverse, spread, dt_wide[2:], bias[2:],
        rate[2:], (skip[2] + skip[3])[None, :], out_weight,
    )
    term = term.reshape(ROWS, owners, OWN_BLK, groups, width)
    term = jnp.transpose(term, (0, 3, 2, 1, 4)).reshape(slots, frames_total * width)[:per_owner]
    return lax.psum_scatter(term, "space", scatter_dimension=1, tiled=True)


def solution(mesh):
    placed = (
        P(("groups", "tm"), "space"),
        P("groups"),
        P("groups"),
        P("groups", None),
        P(),
        P(),
        P(None, "space", None),
        P(None, None, "space"),
        P(None, "space"),
        P(None, "space", None),
        P(None, "space"),
        P("space", None),
    )
    return jax.shard_map(
        body, mesh=mesh, in_specs=placed, out_specs=P("tm", ("groups", "space")), check_vma=False
    )
```

```python
import functools

import jax
import jax.numpy as jnp
import numpy as np
from jax import lax
from jax.experimental import pallas as pl
from jax.experimental.pallas import tpu as pltpu
from jax.sharding import PartitionSpec as P

PATCHES = 196
OWN_BLK = 4
IN_BLK = 8
ROWS = 4
STATE = 16
RANK = 36
HALF = 2 * (RANK + 2 * STATE)
EPSILON = 1e-05
LOG2E = 1.4426950408889634
CLOSED = 1e4
F32 = jnp.float32
BF16 = jnp.bfloat16


def chunks_of(part):
    assert 0 < part % 128 <= 32
    return tuple((512 * i, 512) for i in range(part // 128)) + ((512 * (part // 128), 128),)


def lanes_of(part):
    return 512 * (part // 128) + 128


def constants():
    perm = np.zeros((512, 512), np.float32)
    for r in range(ROWS):
        for ch in range(128):
            perm[r * 128 + ch, (ch // 32) * 128 + r * 32 + ch % 32] = 1
    spread = np.zeros((ROWS * STATE, STATE * 128), np.float32)
    for r in range(ROWS):
        for s in range(STATE):
            spread[r * STATE + s, s * 128 + r * 32 : s * 128 + r * 32 + 32] = 1
    return perm, spread


def widening(part):
    widen = np.zeros((part, lanes_of(part)), np.float32)
    for ch in range(part):
        for r in range(ROWS):
            widen[ch, (ch // 32) * 128 + r * 32 + ch % 32] = 1
    return widen


PERM, SPREAD = constants()


def dot(a, b):
    return jnp.dot(a, b, preferred_element_type=F32)


def pack_rows(wide, tail, perm_ref, chunk, size):
    wide = wide if size == 512 else None
    if wide is not None:
        return dot(jnp.concatenate([wide(r, chunk) for r in range(ROWS)], axis=1), perm_ref[...])
    total = 0.0
    for r in range(ROWS):
        piece = tail(r)
        total = total + dot(piece, perm_ref[128 * r : 128 * r + piece.shape[1], 0:128])
    return total


def store_tiles(ref, k, start, block):
    rows = ref.shape[1]
    flat = ref.reshape(2, rows * STATE, 128)
    for t in range(block.shape[1] // 128):
        flat[k, pl.ds(start // 128 + t, rows, stride=STATE), :] = block[:, 128 * t : 128 * t + 128]


def load_tiles(ref, k, start, size):
    rows = ref.shape[1]
    flat = ref.reshape(2, rows * STATE, 128)
    parts = [flat[k, pl.ds(start // 128 + t, rows, stride=STATE), :] for t in range(size // 128)]
    return jnp.concatenate(parts, axis=1)


def prepare(part, values, stats_ref, base, closed, weights, scratch):
    perm_ref, spread_ref, dt_ref, bias_ref = weights
    u_ref, d_ref, x_ref, b_ref, c_ref = scratch
    wide, tail = values
    stats = [stats_ref[r, :, base : base + HALF].astype(F32) for r in range(ROWS)]
    for k in range(2):
        low = jnp.concatenate([s[:, RANK * k : RANK * k + RANK] for s in stats], axis=1).astype(BF16)
        for chunk, (start, size) in enumerate(chunks_of(part)):
            cols = slice(start, start + size)
            if k == 0:
                u_ref[:, cols] = pack_rows(wide, tail, perm_ref, chunk, size)
            delta = dot(low, dt_ref[k, :, cols]) + bias_ref[k, :, cols]
            delta = jnp.maximum(delta, 0.0) + jnp.log1p(jnp.exp(-jnp.abs(delta)))
            store_tiles(x_ref, k, start, delta * u_ref[:, cols])
            if closed is not None:
                delta = jnp.where(closed[k] > 0.0, CLOSED, delta)
            store_tiles(d_ref, k, start, delta)
        for which, out_ref in ((0, b_ref), (1, c_ref)):
            at = 2 * RANK + STATE * (2 * k + which)
            picked = jnp.concatenate([s[:, at : at + STATE] for s in stats], axis=1).astype(BF16)
            for q in range(4):
                block = dot(picked, spread_ref[:, 512 * q : 512 * q + 512])
                store_tiles(out_ref, k, 512 * q, block)


def scan(k, steps, unroll, row_of, scratch, rate_ref, y_ref):
    u_ref, d_ref, x_ref, b_ref, c_ref = scratch
    tiles = u_ref.shape[1] // 128

    def step(i, state):
        row = row_of(i)
        b_now = b_ref[k, row]
        c_now = c_ref[k, row]
        after = []
        for t in range(tiles):
            cols = slice(128 * t, 128 * t + 128)
            d_now = jnp.broadcast_to(d_ref[k, row, t : t + 1, :], (STATE, 128))
            x_now = jnp.broadcast_to(x_ref[k, row, t : t + 1, :], (STATE, 128))
            h = jnp.exp2(d_now * rate_ref[k, :, cols]) * state[t] + x_now * b_now
            y_ref[k, row, t : t + 1, :] = jnp.sum(h * c_now, axis=0, keepdims=True)
            after.append(h)
        return tuple(after)

    start = tuple(jnp.zeros((STATE, 128), F32) for _ in range(tiles))
    lax.fori_loop(0, steps, step, start, unroll=unroll)


def silu(v):
    return v * jax.nn.sigmoid(v)


def first_kernel(
    x_ref, w_ref, all_ref, gain_ref, proj_ref, pick_ref, inner_ref, stats_ref, tiles_ref, gate_ref
):
    x = x_ref[0].astype(F32)
    scale = lax.rsqrt(jnp.mean(x * x, axis=1, keepdims=True) + EPSILON)
    normed = (x * scale * gain_ref[...]).astype(BF16)
    part = inner_ref.shape[2]
    inner = silu(dot(normed, w_ref[0])).astype(BF16)
    gate = dot(normed, w_ref[1]).astype(BF16)
    inner_ref[0] = inner
    whole = silu(dot(normed, all_ref[0])).astype(BF16)
    stats = dot(whole, proj_ref[...]).astype(BF16)
    stats_ref[0] = stats[:, :HALF]
    pick = pick_ref[...]
    tiles_ref[0, :, :part] = dot(pick, inner).astype(BF16)
    tiles_ref[0, :, part:] = dot(pick, stats[:, HALF:]).astype(BF16)
    gate_ref[0] = dot(pick, gate).astype(BF16)


def spatial_kernel(
    inner_ref, stats_ref, gate_ref, pick_ref, perm_ref, inverse_ref, spread_ref, dt_ref, bias_ref, rate_ref,
    skip_ref, out_ref, u_ref, d_ref, x_ref, b_ref, c_ref, y_ref
):
    scratch = (u_ref, d_ref, x_ref, b_ref, c_ref)
    length, part = u_ref.shape[0], inner_ref.shape[2]
    cut = part // 128 * 128
    tail = part - cut
    values = (
        lambda r, c: inner_ref[r, :, 128 * c : 128 * c + 128],
        lambda r: inner_ref[r, :, cut:],
    )
    prepare(part, values, stats_ref, 0, None, (perm_ref, spread_ref, dt_ref, bias_ref), scratch)
    scan(0, length, 4, lambda i: i, scratch, rate_ref, y_ref)
    scan(1, length, 4, lambda i: length - 1 - i, scratch, rate_ref, y_ref)
    pick = pick_ref[...]
    for start, size in chunks_of(part):
        cols = slice(start, start + size)
        total = load_tiles(y_ref, 0, start, size) + load_tiles(y_ref, 1, start, size)
        total = total + skip_ref[:, cols] * u_ref[:, cols]
        total = dot(pick, total.astype(BF16)).astype(BF16)
        if size == 512:
            back = dot(total, inverse_ref[...]).astype(BF16)
            for r in range(ROWS):
                at = start // 4
                out_ref[r, :, at : at + 128] = back[:, 128 * r : 128 * r + 128]
        else:
            for r in range(ROWS):
                back = dot(total, inverse_ref[0:128, 128 * r : 128 * r + tail])
                out_ref[r, :, 2 * cut : 2 * cut + tail] = back.astype(BF16)
    for r in range(ROWS):
        out_ref[r, :, cut : 2 * cut] = gate_ref[r, :, :cut]
        out_ref[r, :, 2 * cut + tail :] = gate_ref[r, :, cut:]


def temporal_kernel(
    frames, groups, part, moved_ref, closed_ref, perm_ref, spread_ref, dt_ref, bias_ref, rate_ref,
    skip_ref, out_ref, u_ref, d_ref, x_ref, b_ref, c_ref, y_ref
):
    scratch = (u_ref, d_ref, x_ref, b_ref, c_ref)
    owners = frames // OWN_BLK
    cut = part // 128 * 128
    values = (
        lambda r, c: moved_ref[r, :, 128 * c : 128 * c + 128],
        lambda r: moved_ref[r, :, cut:part],
    )
    closed = (closed_ref[:, 0:1], closed_ref[:, 1:2])
    prepare(part, values, moved_ref, part, closed, (perm_ref, spread_ref, dt_ref, bias_ref), scratch)

    def row_at(i, backward):
        group, frame = i // frames, i % frames
        if backward:
            frame = frames - 1 - frame
        return ((frame % owners) * OWN_BLK + frame // owners) * groups + group

    steps = frames * groups
    scan(0, steps, 4, lambda i: row_at(i, False), scratch, rate_ref, y_ref)
    scan(1, steps, 4, lambda i: row_at(i, True), scratch, rate_ref, y_ref)
    for start, size in chunks_of(part):
        cols = slice(start, start + size)
        total = load_tiles(y_ref, 0, start, size) + load_tiles(y_ref, 1, start, size)
        out_ref[:, cols] = total + skip_ref[:, cols] * u_ref[:, cols]


def output_kernel(temporal_ref, moved_ref, perm_ref, inverse_ref, w_ref, out_ref):
    part = w_ref.shape[0]
    cut = part // 128 * 128
    tail = part - cut
    spatial = (
        lambda r, c: moved_ref[r, :, 128 * c : 128 * c + 128],
        lambda r: moved_ref[r, :, 2 * cut : 2 * cut + tail],
    )
    gate = (
        lambda r, c: moved_ref[r, :, cut + 128 * c : cut + 128 * c + 128],
        lambda r: moved_ref[r, :, 2 * cut + tail :],
    )
    backs = []
    for chunk, (start, size) in enumerate(chunks_of(part)):
        total = temporal_ref[:, start : start + size] + pack_rows(*spatial, perm_ref, chunk, size)
        total = (total * silu(pack_rows(*gate, perm_ref, chunk, size))).astype(BF16)
        if size == 512:
            total = dot(total, inverse_ref[...]).astype(BF16)
        backs.append(total)
    for r in range(ROWS):
        lanes = slice(128 * r, 128 * r + 128)
        last = dot(backs[-1], inverse_ref[0:128, 128 * r : 128 * r + tail]).astype(BF16)
        term = dot(last, w_ref[cut:, :])
        for c in range(cut // 128):
            term = term + dot(backs[c][:, lanes], w_ref[128 * c : 128 * c + 128, :])
        out_ref[r] = term.astype(BF16)


def scan_scratch(rows, part):
    return [pltpu.VMEM((rows, lanes_of(part)), F32)] + [pltpu.VMEM((2, rows, STATE, 128), F32)] * 5


def call(kernel, out_shape, scratch, flops, *operands):
    return pl.pallas_call(
        kernel,
        out_shape=out_shape,
        in_specs=[pl.BlockSpec(memory_space=pltpu.VMEM)] * len(operands),
        out_specs=pl.BlockSpec(memory_space=pltpu.VMEM),
        scratch_shapes=scratch,
        compiler_params=pltpu.CompilerParams(vmem_limit_bytes=56 * 1024 * 1024),
        cost_estimate=pl.CostEstimate(flops=flops, bytes_accessed=8_000_000, transcendentals=7_000_000),
    )(*operands)


def body(
    frames_in, arrive_len, clip_len, tile_pick, norm_gain, in_weight, proj_weight, dt_weight, dt_bias,
    decay_rate, skip_gain, out_weight
):
    owners = lax.axis_size("tm")
    my_owner = lax.axis_index("tm")
    space_index = lax.axis_index("space")
    patches = PATCHES
    width = in_weight.shape[1]
    part = out_weight.shape[0]
    frames_total = owners * OWN_BLK
    per_owner = tile_pick.shape[1] // owners
    groups = -(-per_owner // ROWS)
    slots = ROWS * groups

    weight = lax.dynamic_slice_in_dim(in_weight, space_index * part, part, 2)
    widen = jnp.asarray(widening(part))
    exact = functools.partial(
        jnp.einsum, precision=lax.Precision.HIGHEST, preferred_element_type=F32
    )
    rate = exact("kcs,cn->ksn", decay_rate, widen) * -LOG2E
    bias = exact("kc,cn->kn", dt_bias, widen)[:, None, :]
    skip = exact("kc,cn->kn", skip_gain, widen)
    dt_wide = jnp.einsum(
        "kic,cn->kin", dt_weight, widen.astype(BF16), preferred_element_type=F32
    ).astype(BF16)
    lane_row = (jnp.arange(lanes_of(part), dtype=jnp.int32) % 128) // 32
    same = (lane_row[None, :] == jnp.arange(ROWS, dtype=jnp.int32)[:, None])[None, :, None, :]
    dt_wide = jnp.where(same, dt_wide[:, None], jnp.zeros((), BF16)).reshape(4, ROWS * RANK, lanes_of(part))
    pieces = []
    for half in (0, 2):
        pieces += [proj_weight[half, :, :RANK], proj_weight[half + 1, :, :RANK]]
        pieces += [proj_weight[half, :, RANK:], proj_weight[half + 1, :, RANK:]]
    proj = jnp.concatenate(pieces, axis=1)
    spaces = lax.axis_size("space")
    shares = [proj] + [
        lax.ppermute(proj, "space", [(i, (i + k) % spaces) for i in range(spaces)])
        for k in range(1, spaces)
    ]
    order = (space_index - jnp.arange(spaces, dtype=jnp.int32)) % spaces
    proj = jnp.take(jnp.stack(shares), order, axis=0).reshape(spaces * part, 2 * HALF)
    pick = tile_pick.astype(BF16).T.reshape(owners, per_owner, patches)
    pick = jnp.pad(pick, ((0, 0), (0, slots - per_owner), (0, 0))).reshape(owners * slots, patches)
    perm, inverse = jnp.asarray(PERM, BF16), jnp.asarray(PERM.T, BF16)
    spread = jnp.asarray(SPREAD, BF16)

    capacity = (IN_BLK + owners - 1) // owners
    offsets = jnp.cumsum(arrive_len) - arrive_len
    lane_index = jnp.arange(capacity, dtype=jnp.int32)[None, :]
    target_ids = jnp.arange(owners, dtype=jnp.int32)[:, None]
    slot_index = (target_ids - offsets[my_owner]) % owners + lane_index * owners
    packed = jnp.take(frames_in, jnp.minimum(slot_index, IN_BLK - 1).reshape(-1), axis=0)
    arrived = lax.all_to_all(packed, "tm", split_axis=0, concat_axis=0, tiled=True)
    wanted = jnp.arange(OWN_BLK, dtype=jnp.int32) * owners + my_owner
    sender = jnp.sum((offsets[None, :] <= wanted[:, None]).astype(jnp.int32), axis=1) - 1
    lane_of = (wanted - offsets[sender]) // owners
    owned = jnp.take(arrived, sender * capacity + lane_of, axis=0)
    full = lax.all_gather(owned, "space", axis=1, tiled=True).reshape(OWN_BLK, patches, width)

    def per_frame(*dims):
        return pl.BlockSpec((1,) + dims, lambda i: (i, 0, 0))

    def same_each(array):
        return pl.BlockSpec(array.shape, lambda i: (0,) * array.ndim)

    rests = (weight, in_weight, norm_gain[None, :], proj, pick)
    inner, stats, tiles, gate = pl.pallas_call(
        first_kernel,
        grid=(OWN_BLK,),
        out_shape=(
            jax.ShapeDtypeStruct((OWN_BLK, patches, part), BF16),
            jax.ShapeDtypeStruct((OWN_BLK, patches, HALF), BF16),
            jax.ShapeDtypeStruct((OWN_BLK, owners * slots, part + HALF), BF16),
            jax.ShapeDtypeStruct((OWN_BLK, owners * slots, part), BF16),
        ),
        in_specs=[per_frame(patches, width), same_each(weight)]
        + [pl.BlockSpec((1,) + in_weight.shape[1:], lambda i: (0, 0, 0))]
        + [same_each(a) for a in rests[2:]],
        out_specs=(
            per_frame(patches, part),
            per_frame(patches, HALF),
            per_frame(owners * slots, part + HALF),
            per_frame(owners * slots, part),
        ),
        compiler_params=pltpu.CompilerParams(vmem_limit_bytes=40 * 1024 * 1024),
        cost_estimate=pl.CostEstimate(
            flops=4_000_000_000, bytes_accessed=4_000_000, transcendentals=1_000_000
        ),
    )(full, *rests)

    def to_owner(array):
        moved = lax.all_to_all(array, "tm", split_axis=1, concat_axis=0, tiled=True)
        moved = moved.reshape(frames_total, ROWS, groups, array.shape[-1])
        return jnp.swapaxes(moved, 0, 1).reshape(ROWS, frames_total * groups, array.shape[-1])

    early = to_owner(tiles)
    late = call(
        spatial_kernel,
        jax.ShapeDtypeStruct((OWN_BLK, owners * slots, 2 * part), BF16),
        scan_scratch(patches, part),
        20_000_000_000,
        inner, stats, gate, pick, perm, inverse, spread, dt_wide[:2], bias[:2], rate[:2],
        (skip[0] + skip[1])[None, :],
    )
    late = to_owner(late)

    clip_start = jnp.cumsum(clip_len) - clip_len
    row_frame = jnp.arange(frames_total, dtype=jnp.int32)
    row_frame = (row_frame % OWN_BLK) * owners + row_frame // OWN_BLK
    opens = jnp.any(row_frame[:, None] == clip_start[None, :], axis=1) | (row_frame == 0)
    closes = jnp.any(row_frame[:, None] == (clip_start + clip_len - 1)[None, :], axis=1)
    closes = closes | (row_frame == frames_total - 1)
    closed = jnp.stack([opens, closes], axis=1).astype(F32)
    closed = jnp.repeat(closed, groups, axis=0)
    rows = frames_total * groups
    temporal = call(
        functools.partial(temporal_kernel, frames_total, groups, part),
        jax.ShapeDtypeStruct((rows, lanes_of(part)), F32),
        scan_scratch(rows, part),
        20_000_000_000,
        early, closed, perm, spread, dt_wide[2:], bias[2:], rate[2:], (skip[2] + skip[3])[None, :],
    )
    term = call(
        output_kernel,
        jax.ShapeDtypeStruct((ROWS, rows, width), BF16),
        [],
        2_000_000_000,
        temporal, late, perm, inverse, out_weight,
    )
    term = term.reshape(ROWS, owners, OWN_BLK, groups, width)
    term = jnp.transpose(term, (2, 1, 0, 3, 4)).reshape(frames_total, slots, width)[:, :per_owner]
    term = term.reshape(spaces, frames_total // spaces, per_owner, width)
    term = lax.all_to_all(term, "space", split_axis=0, concat_axis=0, tiled=True)
    mixed = jnp.sum(term.astype(F32), axis=0).astype(BF16)
    return jnp.swapaxes(mixed, 0, 1).reshape(per_owner, frames_total // spaces * width)


def solution(mesh):
    placed = (
        P(("groups", "tm"), "space"),
        P("groups"),
        P("groups"),
        P("groups", None),
        P(),
        P(),
        P(None, "space", None),
        P(None, None, "space"),
        P(None, "space"),
        P(None, "space", None),
        P(None, "space"),
        P("space", None),
    )
    return jax.shard_map(
        body, mesh=mesh, in_specs=placed, out_specs=P("tm", ("groups", "space")), check_vma=False
    )
```

```python
import functools

import jax
import jax.numpy as jnp
import numpy as np
from jax import lax
from jax.experimental import pallas as pl
from jax.experimental.pallas import tpu as pltpu
from jax.sharding import PartitionSpec as P

PATCHES = 196
OWN_BLK = 4
IN_BLK = 8
ROWS = 4
STATE = 16
RANK = 36
HALF = 2 * (RANK + 2 * STATE)
EPSILON = 1e-05
LOG2E = 1.4426950408889634
CLOSED = 1e4
F32 = jnp.float32
BF16 = jnp.bfloat16


def chunks_of(part):
    assert 0 < part % 128 <= 32
    return tuple((512 * i, 512) for i in range(part // 128)) + ((512 * (part // 128), 128),)


def lanes_of(part):
    return 512 * (part // 128) + 128


def constants():
    perm = np.zeros((512, 512), np.float32)
    for r in range(ROWS):
        for ch in range(128):
            perm[r * 128 + ch, (ch // 32) * 128 + r * 32 + ch % 32] = 1
    spread = np.zeros((ROWS * STATE, STATE * 128), np.float32)
    for r in range(ROWS):
        for s in range(STATE):
            spread[r * STATE + s, s * 128 + r * 32 : s * 128 + r * 32 + 32] = 1
    return perm, spread


def widening(part):
    widen = np.zeros((part, lanes_of(part)), np.float32)
    for ch in range(part):
        for r in range(ROWS):
            widen[ch, (ch // 32) * 128 + r * 32 + ch % 32] = 1
    return widen


PERM, SPREAD = constants()


def dot(a, b):
    return jnp.dot(a, b, preferred_element_type=F32)


def pack_rows(wide, tail, perm_ref, chunk, size):
    wide = wide if size == 512 else None
    if wide is not None:
        return dot(jnp.concatenate([wide(r, chunk) for r in range(ROWS)], axis=1), perm_ref[...])
    total = 0.0
    for r in range(ROWS):
        piece = tail(r)
        total = total + dot(piece, perm_ref[128 * r : 128 * r + piece.shape[1], 0:128])
    return total


def store_tiles(ref, k, start, block):
    rows = ref.shape[1]
    flat = ref.reshape(2, rows * STATE, 128)
    for t in range(block.shape[1] // 128):
        flat[k, pl.ds(start // 128 + t, rows, stride=STATE), :] = block[:, 128 * t : 128 * t + 128]


def load_tiles(ref, k, start, size):
    rows = ref.shape[1]
    flat = ref.reshape(2, rows * STATE, 128)
    parts = [flat[k, pl.ds(start // 128 + t, rows, stride=STATE), :] for t in range(size // 128)]
    return jnp.concatenate(parts, axis=1)


def prepare(part, values, stats_ref, base, closed, weights, scratch):
    perm_ref, spread_ref, dt_ref, bias_ref = weights
    u_ref, d_ref, x_ref, b_ref, c_ref = scratch
    wide, tail = values
    stats = [stats_ref[r, :, base : base + HALF].astype(F32) for r in range(ROWS)]
    for k in range(2):
        low = jnp.concatenate([s[:, RANK * k : RANK * k + RANK] for s in stats], axis=1).astype(BF16)
        for chunk, (start, size) in enumerate(chunks_of(part)):
            cols = slice(start, start + size)
            if k == 0:
                u_ref[:, cols] = pack_rows(wide, tail, perm_ref, chunk, size)
            delta = dot(low, dt_ref[k, :, cols]) + bias_ref[k, :, cols]
            delta = jnp.maximum(delta, 0.0) + jnp.log1p(jnp.exp(-jnp.abs(delta)))
            store_tiles(x_ref, k, start, delta * u_ref[:, cols])
            if closed is not None:
                delta = jnp.where(closed[k] > 0.0, CLOSED, delta)
            store_tiles(d_ref, k, start, delta)
        for which, out_ref in ((0, b_ref), (1, c_ref)):
            at = 2 * RANK + STATE * (2 * k + which)
            picked = jnp.concatenate([s[:, at : at + STATE] for s in stats], axis=1).astype(BF16)
            for q in range(4):
                block = dot(picked, spread_ref[:, 512 * q : 512 * q + 512])
                store_tiles(out_ref, k, 512 * q, block)


def scan(k, steps, unroll, row_of, scratch, rate_ref, y_ref):
    u_ref, d_ref, x_ref, b_ref, c_ref = scratch
    tiles = u_ref.shape[1] // 128

    def step(i, state):
        row = row_of(i)
        b_now = b_ref[k, row]
        c_now = c_ref[k, row]
        after = []
        for t in range(tiles):
            cols = slice(128 * t, 128 * t + 128)
            d_now = jnp.broadcast_to(d_ref[k, row, t : t + 1, :], (STATE, 128))
            x_now = jnp.broadcast_to(x_ref[k, row, t : t + 1, :], (STATE, 128))
            h = jnp.exp2(d_now * rate_ref[k, :, cols]) * state[t] + x_now * b_now
            y_ref[k, row, t : t + 1, :] = jnp.sum(h * c_now, axis=0, keepdims=True)
            after.append(h)
        return tuple(after)

    start = tuple(jnp.zeros((STATE, 128), F32) for _ in range(tiles))
    lax.fori_loop(0, steps, step, start, unroll=unroll)


def silu(v):
    return v * jax.nn.sigmoid(v)


def first_kernel(
    x_ref, w_ref, all_ref, gain_ref, proj_ref, pick_ref, inner_ref, stats_ref, tiles_ref, gate_ref
):
    x = x_ref[0].astype(F32)
    scale = lax.rsqrt(jnp.mean(x * x, axis=1, keepdims=True) + EPSILON)
    normed = (x * scale * gain_ref[...]).astype(BF16)
    part = inner_ref.shape[2]
    inner = silu(dot(normed, w_ref[0])).astype(BF16)
    gate = dot(normed, w_ref[1]).astype(BF16)
    inner_ref[0] = inner
    whole = silu(dot(normed, all_ref[0])).astype(BF16)
    stats = dot(whole, proj_ref[...]).astype(BF16)
    stats_ref[0] = stats[:, :HALF]
    pick = pick_ref[...]
    tiles_ref[0, :, :part] = dot(pick, inner).astype(BF16)
    tiles_ref[0, :, part:] = dot(pick, stats[:, HALF:]).astype(BF16)
    gate_ref[0] = dot(pick, gate).astype(BF16)


def spatial_kernel(
    inner_ref, stats_ref, gate_ref, pick_ref, perm_ref, inverse_ref, spread_ref, dt_ref, bias_ref, rate_ref,
    skip_ref, out_ref, u_ref, d_ref, x_ref, b_ref, c_ref, y_ref
):
    scratch = (u_ref, d_ref, x_ref, b_ref, c_ref)
    length, part = u_ref.shape[0], inner_ref.shape[2]
    cut = part // 128 * 128
    tail = part - cut
    values = (
        lambda r, c: inner_ref[r, :, 128 * c : 128 * c + 128],
        lambda r: inner_ref[r, :, cut:],
    )
    prepare(part, values, stats_ref, 0, None, (perm_ref, spread_ref, dt_ref, bias_ref), scratch)
    scan(0, length, 4, lambda i: i, scratch, rate_ref, y_ref)
    scan(1, length, 4, lambda i: length - 1 - i, scratch, rate_ref, y_ref)
    pick = pick_ref[...]
    for start, size in chunks_of(part):
        cols = slice(start, start + size)
        total = load_tiles(y_ref, 0, start, size) + load_tiles(y_ref, 1, start, size)
        total = total + skip_ref[:, cols] * u_ref[:, cols]
        total = dot(pick, total.astype(BF16)).astype(BF16)
        if size == 512:
            back = dot(total, inverse_ref[...]).astype(BF16)
            for r in range(ROWS):
                at = start // 4
                out_ref[r, :, at : at + 128] = back[:, 128 * r : 128 * r + 128]
        else:
            for r in range(ROWS):
                back = dot(total, inverse_ref[0:128, 128 * r : 128 * r + tail])
                out_ref[r, :, 2 * cut : 2 * cut + tail] = back.astype(BF16)
    for r in range(ROWS):
        out_ref[r, :, cut : 2 * cut] = gate_ref[r, :, :cut]
        out_ref[r, :, 2 * cut + tail :] = gate_ref[r, :, cut:]


def temporal_kernel(
    frames, groups, part, moved_ref, closed_ref, perm_ref, spread_ref, dt_ref, bias_ref, rate_ref,
    skip_ref, out_ref, u_ref, d_ref, x_ref, b_ref, c_ref, y_ref
):
    scratch = (u_ref, d_ref, x_ref, b_ref, c_ref)
    owners = frames // OWN_BLK
    cut = part // 128 * 128
    values = (
        lambda r, c: moved_ref[r, :, 128 * c : 128 * c + 128],
        lambda r: moved_ref[r, :, cut:part],
    )
    closed = (closed_ref[:, 0:1], closed_ref[:, 1:2])
    prepare(part, values, moved_ref, part, closed, (perm_ref, spread_ref, dt_ref, bias_ref), scratch)

    def row_at(i, backward):
        group, frame = i // frames, i % frames
        if backward:
            frame = frames - 1 - frame
        return ((frame % owners) * OWN_BLK + frame // owners) * groups + group

    steps = frames * groups
    scan(0, steps, 4, lambda i: row_at(i, False), scratch, rate_ref, y_ref)
    scan(1, steps, 4, lambda i: row_at(i, True), scratch, rate_ref, y_ref)
    for start, size in chunks_of(part):
        cols = slice(start, start + size)
        total = load_tiles(y_ref, 0, start, size) + load_tiles(y_ref, 1, start, size)
        out_ref[:, cols] = total + skip_ref[:, cols] * u_ref[:, cols]


def output_kernel(temporal_ref, moved_ref, perm_ref, inverse_ref, w_ref, out_ref):
    part = w_ref.shape[0]
    cut = part // 128 * 128
    tail = part - cut
    spatial = (
        lambda r, c: moved_ref[r, :, 128 * c : 128 * c + 128],
        lambda r: moved_ref[r, :, 2 * cut : 2 * cut + tail],
    )
    gate = (
        lambda r, c: moved_ref[r, :, cut + 128 * c : cut + 128 * c + 128],
        lambda r: moved_ref[r, :, 2 * cut + tail :],
    )
    backs = []
    for chunk, (start, size) in enumerate(chunks_of(part)):
        total = temporal_ref[:, start : start + size] + pack_rows(*spatial, perm_ref, chunk, size)
        total = (total * silu(pack_rows(*gate, perm_ref, chunk, size))).astype(BF16)
        if size == 512:
            total = dot(total, inverse_ref[...]).astype(BF16)
        backs.append(total)
    for r in range(ROWS):
        lanes = slice(128 * r, 128 * r + 128)
        last = dot(backs[-1], inverse_ref[0:128, 128 * r : 128 * r + tail]).astype(BF16)
        term = dot(last, w_ref[cut:, :])
        for c in range(cut // 128):
            term = term + dot(backs[c][:, lanes], w_ref[128 * c : 128 * c + 128, :])
        out_ref[r] = term.astype(BF16)


def scan_scratch(rows, part):
    return [pltpu.VMEM((rows, lanes_of(part)), F32)] + [pltpu.VMEM((2, rows, STATE, 128), F32)] * 5


def call(kernel, out_shape, scratch, flops, *operands):
    return pl.pallas_call(
        kernel,
        out_shape=out_shape,
        in_specs=[pl.BlockSpec(memory_space=pltpu.VMEM)] * len(operands),
        out_specs=pl.BlockSpec(memory_space=pltpu.VMEM),
        scratch_shapes=scratch,
        compiler_params=pltpu.CompilerParams(vmem_limit_bytes=56 * 1024 * 1024),
        cost_estimate=pl.CostEstimate(flops=flops, bytes_accessed=8_000_000, transcendentals=7_000_000),
    )(*operands)


def body(
    frames_in, arrive_len, clip_len, tile_pick, norm_gain, in_weight, proj_weight, dt_weight, dt_bias,
    decay_rate, skip_gain, out_weight
):
    owners = lax.axis_size("tm")
    my_owner = lax.axis_index("tm")
    space_index = lax.axis_index("space")
    patches = PATCHES
    width = in_weight.shape[1]
    part = out_weight.shape[0]
    frames_total = owners * OWN_BLK
    per_owner = tile_pick.shape[1] // owners
    groups = -(-per_owner // ROWS)
    slots = ROWS * groups

    weight = lax.dynamic_slice_in_dim(in_weight, space_index * part, part, 2)
    widen = jnp.asarray(widening(part))
    exact = functools.partial(
        jnp.einsum, precision=lax.Precision.HIGHEST, preferred_element_type=F32
    )
    rate = exact("kcs,cn->ksn", decay_rate, widen) * -LOG2E
    bias = exact("kc,cn->kn", dt_bias, widen)[:, None, :]
    skip = exact("kc,cn->kn", skip_gain, widen)
    dt_wide = jnp.einsum(
        "kic,cn->kin", dt_weight, widen.astype(BF16), preferred_element_type=F32
    ).astype(BF16)
    lane_row = (jnp.arange(lanes_of(part), dtype=jnp.int32) % 128) // 32
    same = (lane_row[None, :] == jnp.arange(ROWS, dtype=jnp.int32)[:, None])[None, :, None, :]
    dt_wide = jnp.where(same, dt_wide[:, None], jnp.zeros((), BF16)).reshape(4, ROWS * RANK, lanes_of(part))
    pick = tile_pick.astype(BF16).T.reshape(owners, per_owner, patches)
    pick = jnp.pad(pick, ((0, 0), (0, slots - per_owner), (0, 0))).reshape(owners * slots, patches)
    perm, inverse = jnp.asarray(PERM, BF16), jnp.asarray(PERM.T, BF16)
    spread = jnp.asarray(SPREAD, BF16)

    capacity = (IN_BLK + owners - 1) // owners
    offsets = jnp.cumsum(arrive_len) - arrive_len
    lane_index = jnp.arange(capacity, dtype=jnp.int32)[None, :]
    target_ids = jnp.arange(owners, dtype=jnp.int32)[:, None]
    slot_index = (target_ids - offsets[my_owner]) % owners + lane_index * owners
    packed = jnp.take(frames_in, jnp.minimum(slot_index, IN_BLK - 1).reshape(-1), axis=0)
    packed, proj_weight = lax.optimization_barrier((packed, proj_weight))
    arrived = lax.all_to_all(packed, "tm", split_axis=0, concat_axis=0, tiled=True)
    pieces = []
    for half in (0, 2):
        pieces += [proj_weight[half, :, :RANK], proj_weight[half + 1, :, :RANK]]
        pieces += [proj_weight[half, :, RANK:], proj_weight[half + 1, :, RANK:]]
    proj = jnp.concatenate(pieces, axis=1)
    spaces = lax.axis_size("space")
    order = (space_index - jnp.arange(spaces, dtype=jnp.int32)) % spaces

    def to_next(array, k):
        return lax.ppermute(array, "space", [(i, (i + k) % spaces) for i in range(spaces)])

    def gathered(array):
        shares = [array] + [to_next(array, k) for k in range(1, spaces)]
        return jnp.take(jnp.stack(shares), order, axis=0)

    proj = gathered(proj).reshape(spaces * part, 2 * HALF)
    wanted = jnp.arange(OWN_BLK, dtype=jnp.int32) * owners + my_owner
    sender = jnp.sum((offsets[None, :] <= wanted[:, None]).astype(jnp.int32), axis=1) - 1
    lane_of = (wanted - offsets[sender]) // owners
    owned = jnp.take(arrived, sender * capacity + lane_of, axis=0)
    full = jnp.swapaxes(gathered(owned), 0, 1).reshape(OWN_BLK, patches, width)

    def per_frame(*dims):
        return pl.BlockSpec((1,) + dims, lambda i: (i, 0, 0))

    def same_each(array):
        return pl.BlockSpec(array.shape, lambda i: (0,) * array.ndim)

    rests = (weight, in_weight, norm_gain[None, :], proj, pick)
    inner, stats, tiles, gate = pl.pallas_call(
        first_kernel,
        grid=(OWN_BLK,),
        out_shape=(
            jax.ShapeDtypeStruct((OWN_BLK, patches, part), BF16),
            jax.ShapeDtypeStruct((OWN_BLK, patches, HALF), BF16),
            jax.ShapeDtypeStruct((OWN_BLK, owners * slots, part + HALF), BF16),
            jax.ShapeDtypeStruct((OWN_BLK, owners * slots, part), BF16),
        ),
        in_specs=[per_frame(patches, width), same_each(weight)]
        + [pl.BlockSpec((1,) + in_weight.shape[1:], lambda i: (0, 0, 0))]
        + [same_each(a) for a in rests[2:]],
        out_specs=(
            per_frame(patches, part),
            per_frame(patches, HALF),
            per_frame(owners * slots, part + HALF),
            per_frame(owners * slots, part),
        ),
        compiler_params=pltpu.CompilerParams(vmem_limit_bytes=40 * 1024 * 1024),
        cost_estimate=pl.CostEstimate(
            flops=4_000_000_000, bytes_accessed=4_000_000, transcendentals=1_000_000
        ),
    )(full, *rests)

    def to_owner(array):
        moved = lax.all_to_all(array, "tm", split_axis=1, concat_axis=0, tiled=True)
        moved = moved.reshape(frames_total, ROWS, groups, array.shape[-1])
        return jnp.swapaxes(moved, 0, 1).reshape(ROWS, frames_total * groups, array.shape[-1])

    early = to_owner(tiles)
    late = call(
        spatial_kernel,
        jax.ShapeDtypeStruct((OWN_BLK, owners * slots, 2 * part), BF16),
        scan_scratch(patches, part),
        20_000_000_000,
        inner, stats, gate, pick, perm, inverse, spread, dt_wide[:2], bias[:2], rate[:2],
        (skip[0] + skip[1])[None, :],
    )
    late = to_owner(late)

    clip_start = jnp.cumsum(clip_len) - clip_len
    row_frame = jnp.arange(frames_total, dtype=jnp.int32)
    row_frame = (row_frame % OWN_BLK) * owners + row_frame // OWN_BLK
    opens = jnp.any(row_frame[:, None] == clip_start[None, :], axis=1) | (row_frame == 0)
    closes = jnp.any(row_frame[:, None] == (clip_start + clip_len - 1)[None, :], axis=1)
    closes = closes | (row_frame == frames_total - 1)
    closed = jnp.stack([opens, closes], axis=1).astype(F32)
    closed = jnp.repeat(closed, groups, axis=0)
    rows = frames_total * groups
    temporal = call(
        functools.partial(temporal_kernel, frames_total, groups, part),
        jax.ShapeDtypeStruct((rows, lanes_of(part)), F32),
        scan_scratch(rows, part),
        20_000_000_000,
        early, closed, perm, spread, dt_wide[2:], bias[2:], rate[2:], (skip[2] + skip[3])[None, :],
    )
    term = call(
        output_kernel,
        jax.ShapeDtypeStruct((ROWS, rows, width), BF16),
        [],
        2_000_000_000,
        temporal, late, perm, inverse, out_weight,
    )
    term = term.reshape(ROWS, owners, OWN_BLK, groups, width)
    term = jnp.transpose(term, (2, 1, 0, 3, 4)).reshape(frames_total, slots, width)[:, :per_owner]
    term = term.reshape(spaces, frames_total // spaces, per_owner, width)
    mixed = 0.0
    for k in range(spaces):
        piece = lax.dynamic_index_in_dim(term, (space_index + k) % spaces, 0, keepdims=False)
        mixed = mixed + (to_next(piece, k) if k else piece).astype(F32)
    mixed = mixed.astype(BF16)
    return jnp.swapaxes(mixed, 0, 1).reshape(per_owner, frames_total // spaces * width)


def solution(mesh):
    placed = (
        P(("groups", "tm"), "space"),
        P("groups"),
        P("groups"),
        P("groups", None),
        P(),
        P(),
        P(None, "space", None),
        P(None, None, "space"),
        P(None, "space"),
        P(None, "space", None),
        P(None, "space"),
        P("space", None),
    )
    return jax.shard_map(
        body, mesh=mesh, in_specs=placed, out_specs=P("tm", ("groups", "space")), check_vma=False
    )
```

```python
import functools

import jax
import jax.numpy as jnp
import numpy as np
from jax import lax
from jax.experimental import pallas as pl
from jax.experimental.pallas import tpu as pltpu
from jax.sharding import PartitionSpec as P

PATCHES = 196
OWN_BLK = 4
IN_BLK = 8
ROWS = 4
STATE = 16
RANK = 36
HALF = 2 * (RANK + 2 * STATE)
EPSILON = 1e-05
LOG2E = 1.4426950408889634
CLOSED = 1e4
F32 = jnp.float32
BF16 = jnp.bfloat16


def chunks_of(part):
    assert 0 < part % 128 <= 32
    return tuple((512 * i, 512) for i in range(part // 128)) + ((512 * (part // 128), 128),)


def lanes_of(part):
    return 512 * (part // 128) + 128


def constants():
    perm = np.zeros((512, 512), np.float32)
    for r in range(ROWS):
        for ch in range(128):
            perm[r * 128 + ch, (ch // 32) * 128 + r * 32 + ch % 32] = 1
    spread = np.zeros((ROWS * STATE, STATE * 128), np.float32)
    for r in range(ROWS):
        for s in range(STATE):
            spread[r * STATE + s, s * 128 + r * 32 : s * 128 + r * 32 + 32] = 1
    return perm, spread


def widening(part):
    widen = np.zeros((part, lanes_of(part)), np.float32)
    for ch in range(part):
        for r in range(ROWS):
            widen[ch, (ch // 32) * 128 + r * 32 + ch % 32] = 1
    return widen


PERM, SPREAD = constants()


def dot(a, b):
    return jnp.dot(a, b, preferred_element_type=F32)


def pack_rows(wide, tail, perm_ref, chunk, size):
    wide = wide if size == 512 else None
    if wide is not None:
        return dot(jnp.concatenate([wide(r, chunk) for r in range(ROWS)], axis=1), perm_ref[...])
    total = 0.0
    for r in range(ROWS):
        piece = tail(r)
        total = total + dot(piece, perm_ref[128 * r : 128 * r + piece.shape[1], 0:128])
    return total


def store_tiles(ref, k, start, block):
    rows = ref.shape[1]
    flat = ref.reshape(2, rows * STATE, 128)
    for t in range(block.shape[1] // 128):
        flat[k, pl.ds(start // 128 + t, rows, stride=STATE), :] = block[:, 128 * t : 128 * t + 128]


def load_sums(ref, start, size):
    rows, each = ref.shape[1], ref.shape[2]
    flat = ref.reshape(2, rows * each, 128)
    parts = []
    for t in range(start // 128, (start + size) // 128):
        terms = [flat[k, pl.ds(8 * t + s, rows, stride=each), :] for k in range(2) for s in range(8)]
        parts.append(sum(terms[1:], terms[0]))
    return jnp.concatenate(parts, axis=1)


def prepare(part, values, stats_ref, base, closed, weights, scratch):
    perm_ref, spread_ref, dt_ref, bias_ref = weights
    u_ref, d_ref, x_ref, b_ref, c_ref = scratch
    wide, tail = values
    stats = [stats_ref[r, :, base : base + HALF].astype(F32) for r in range(ROWS)]
    for k in range(2):
        low = jnp.concatenate([s[:, RANK * k : RANK * k + RANK] for s in stats], axis=1).astype(BF16)
        for chunk, (start, size) in enumerate(chunks_of(part)):
            cols = slice(start, start + size)
            if k == 0:
                u_ref[:, cols] = pack_rows(wide, tail, perm_ref, chunk, size)
            delta = dot(low, dt_ref[k, :, cols]) + bias_ref[k, :, cols]
            delta = jnp.maximum(delta, 0.0) + jnp.log1p(jnp.exp(-jnp.abs(delta)))
            store_tiles(x_ref, k, start, delta * u_ref[:, cols])
            if closed is not None:
                delta = jnp.where(closed[k] > 0.0, CLOSED, delta)
            store_tiles(d_ref, k, start, delta)
        for which, out_ref in ((0, b_ref), (1, c_ref)):
            at = 2 * RANK + STATE * (2 * k + which)
            picked = jnp.concatenate([s[:, at : at + STATE] for s in stats], axis=1).astype(BF16)
            for q in range(4):
                block = dot(picked, spread_ref[:, 512 * q : 512 * q + 512])
                store_tiles(out_ref, k, 512 * q, block)


def scan(k, steps, unroll, row_of, scratch, rate_ref, y_ref):
    u_ref, d_ref, x_ref, b_ref, c_ref = scratch
    tiles = u_ref.shape[1] // 128

    def step(i, state):
        row = row_of(i)
        b_now = b_ref[k, row]
        c_now = c_ref[k, row]
        after = []
        for t in range(tiles):
            cols = slice(128 * t, 128 * t + 128)
            d_now = jnp.broadcast_to(d_ref[k, row, t : t + 1, :], (STATE, 128))
            x_now = jnp.broadcast_to(x_ref[k, row, t : t + 1, :], (STATE, 128))
            h = jnp.exp2(d_now * rate_ref[k, :, cols]) * state[t] + x_now * b_now
            product = h * c_now
            y_ref[k, row, 8 * t : 8 * t + 8, :] = product[0:8] + product[8:16]
            after.append(h)
        return tuple(after)

    start = tuple(jnp.zeros((STATE, 128), F32) for _ in range(tiles))
    lax.fori_loop(0, steps, step, start, unroll=unroll)


def silu(v):
    return v * jax.nn.sigmoid(v)


def first_kernel(
    x_ref, w_ref, all_ref, gain_ref, proj_ref, pick_ref, inner_ref, stats_ref, tiles_ref, gate_ref
):
    x = x_ref[0].astype(F32)
    scale = lax.rsqrt(jnp.mean(x * x, axis=1, keepdims=True) + EPSILON)
    normed = (x * scale * gain_ref[...]).astype(BF16)
    part = inner_ref.shape[2]
    inner = silu(dot(normed, w_ref[0])).astype(BF16)
    gate = dot(normed, w_ref[1]).astype(BF16)
    inner_ref[0] = inner
    whole = silu(dot(normed, all_ref[0])).astype(BF16)
    stats = dot(whole, proj_ref[...]).astype(BF16)
    stats_ref[0] = stats[:, :HALF]
    pick = pick_ref[...]
    tiles_ref[0, :, :part] = dot(pick, inner).astype(BF16)
    tiles_ref[0, :, part:] = dot(pick, stats[:, HALF:]).astype(BF16)
    gate_ref[0] = dot(pick, gate).astype(BF16)


def spatial_kernel(
    inner_ref, stats_ref, gate_ref, pick_ref, perm_ref, inverse_ref, spread_ref, dt_ref, bias_ref, rate_ref,
    skip_ref, out_ref, u_ref, d_ref, x_ref, b_ref, c_ref, y_ref
):
    scratch = (u_ref, d_ref, x_ref, b_ref, c_ref)
    length, part = u_ref.shape[0], inner_ref.shape[2]
    cut = part // 128 * 128
    tail = part - cut
    values = (
        lambda r, c: inner_ref[r, :, 128 * c : 128 * c + 128],
        lambda r: inner_ref[r, :, cut:],
    )
    prepare(part, values, stats_ref, 0, None, (perm_ref, spread_ref, dt_ref, bias_ref), scratch)
    scan(0, length, 4, lambda i: i, scratch, rate_ref, y_ref)
    scan(1, length, 4, lambda i: length - 1 - i, scratch, rate_ref, y_ref)
    pick = pick_ref[...]
    for start, size in chunks_of(part):
        cols = slice(start, start + size)
        total = load_sums(y_ref, start, size)
        total = total + skip_ref[:, cols] * u_ref[:, cols]
        total = dot(pick, total.astype(BF16)).astype(BF16)
        if size == 512:
            back = dot(total, inverse_ref[...]).astype(BF16)
            for r in range(ROWS):
                at = start // 4
                out_ref[r, :, at : at + 128] = back[:, 128 * r : 128 * r + 128]
        else:
            for r in range(ROWS):
                back = dot(total, inverse_ref[0:128, 128 * r : 128 * r + tail])
                out_ref[r, :, 2 * cut : 2 * cut + tail] = back.astype(BF16)
    for r in range(ROWS):
        out_ref[r, :, cut : 2 * cut] = gate_ref[r, :, :cut]
        out_ref[r, :, 2 * cut + tail :] = gate_ref[r, :, cut:]


def temporal_kernel(
    frames, groups, part, moved_ref, closed_ref, perm_ref, spread_ref, dt_ref, bias_ref, rate_ref,
    skip_ref, out_ref, u_ref, d_ref, x_ref, b_ref, c_ref, y_ref
):
    scratch = (u_ref, d_ref, x_ref, b_ref, c_ref)
    owners = frames // OWN_BLK
    cut = part // 128 * 128
    values = (
        lambda r, c: moved_ref[r, :, 128 * c : 128 * c + 128],
        lambda r: moved_ref[r, :, cut:part],
    )
    closed = (closed_ref[:, 0:1], closed_ref[:, 1:2])
    prepare(part, values, moved_ref, part, closed, (perm_ref, spread_ref, dt_ref, bias_ref), scratch)

    def row_at(i, backward):
        group, frame = i // frames, i % frames
        if backward:
            frame = frames - 1 - frame
        return ((frame % owners) * OWN_BLK + frame // owners) * groups + group

    steps = frames * groups
    scan(0, steps, 4, lambda i: row_at(i, False), scratch, rate_ref, y_ref)
    scan(1, steps, 4, lambda i: row_at(i, True), scratch, rate_ref, y_ref)
    for start, size in chunks_of(part):
        cols = slice(start, start + size)
        total = load_sums(y_ref, start, size)
        out_ref[:, cols] = total + skip_ref[:, cols] * u_ref[:, cols]


def output_kernel(temporal_ref, moved_ref, perm_ref, inverse_ref, w_ref, out_ref):
    part = w_ref.shape[0]
    cut = part // 128 * 128
    tail = part - cut
    spatial = (
        lambda r, c: moved_ref[r, :, 128 * c : 128 * c + 128],
        lambda r: moved_ref[r, :, 2 * cut : 2 * cut + tail],
    )
    gate = (
        lambda r, c: moved_ref[r, :, cut + 128 * c : cut + 128 * c + 128],
        lambda r: moved_ref[r, :, 2 * cut + tail :],
    )
    backs = []
    for chunk, (start, size) in enumerate(chunks_of(part)):
        total = temporal_ref[:, start : start + size] + pack_rows(*spatial, perm_ref, chunk, size)
        total = (total * silu(pack_rows(*gate, perm_ref, chunk, size))).astype(BF16)
        if size == 512:
            total = dot(total, inverse_ref[...]).astype(BF16)
        backs.append(total)
    for r in range(ROWS):
        lanes = slice(128 * r, 128 * r + 128)
        last = dot(backs[-1], inverse_ref[0:128, 128 * r : 128 * r + tail]).astype(BF16)
        term = dot(last, w_ref[cut:, :])
        for c in range(cut // 128):
            term = term + dot(backs[c][:, lanes], w_ref[128 * c : 128 * c + 128, :])
        out_ref[r] = term.astype(BF16)


def scan_scratch(rows, part):
    lanes = lanes_of(part)
    inputs = [pltpu.VMEM((2, rows, STATE, 128), F32)] * 4
    return [pltpu.VMEM((rows, lanes), F32)] + inputs + [pltpu.VMEM((2, rows, lanes // 16, 128), F32)]


def call(kernel, out_shape, scratch, flops, *operands):
    specs, arrays = [], []
    for operand in operands:
        array, half = operand if isinstance(operand, tuple) else (operand, None)
        arrays.append(array)
        if half is None:
            specs.append(pl.BlockSpec(memory_space=pltpu.VMEM))
        else:
            specs.append(pl.BlockSpec((2,) + array.shape[1:], functools.partial(lambda h, i: (h, 0, 0), half)))
    return pl.pallas_call(
        kernel,
        grid=(1,),
        out_shape=out_shape,
        in_specs=specs,
        out_specs=pl.BlockSpec(memory_space=pltpu.VMEM),
        scratch_shapes=scratch,
        compiler_params=pltpu.CompilerParams(vmem_limit_bytes=56 * 1024 * 1024),
        cost_estimate=pl.CostEstimate(flops=flops, bytes_accessed=8_000_000, transcendentals=7_000_000),
    )(*arrays)


def body(
    frames_in, arrive_len, clip_len, tile_pick, norm_gain, in_weight, proj_weight, dt_weight, dt_bias,
    decay_rate, skip_gain, out_weight
):
    owners = lax.axis_size("tm")
    my_owner = lax.axis_index("tm")
    space_index = lax.axis_index("space")
    patches = PATCHES
    width = in_weight.shape[1]
    part = out_weight.shape[0]
    frames_total = owners * OWN_BLK
    per_owner = tile_pick.shape[1] // owners
    groups = -(-per_owner // ROWS)
    slots = ROWS * groups

    weight = lax.dynamic_slice_in_dim(in_weight, space_index * part, part, 2)
    widen = jnp.asarray(widening(part))
    exact = functools.partial(
        jnp.einsum, precision=lax.Precision.HIGHEST, preferred_element_type=F32
    )
    rate = exact("kcs,cn->ksn", decay_rate, widen) * -LOG2E
    bias = exact("kc,cn->kn", dt_bias, widen)[:, None, :]
    skip = exact("kc,cn->kn", skip_gain, widen)
    dt_wide = jnp.einsum(
        "kic,cn->kin", dt_weight, widen.astype(BF16), preferred_element_type=F32
    ).astype(BF16)
    lane_row = (jnp.arange(lanes_of(part), dtype=jnp.int32) % 128) // 32
    same = (lane_row[None, :] == jnp.arange(ROWS, dtype=jnp.int32)[:, None])[None, :, None, :]
    dt_wide = jnp.where(same, dt_wide[:, None], jnp.zeros((), BF16)).reshape(4, ROWS * RANK, lanes_of(part))
    pick = tile_pick.astype(BF16).T.reshape(owners, per_owner, patches)
    pick = jnp.pad(pick, ((0, 0), (0, slots - per_owner), (0, 0))).reshape(owners * slots, patches)
    perm, inverse = jnp.asarray(PERM, BF16), jnp.asarray(PERM.T, BF16)
    spread = jnp.asarray(SPREAD, BF16)

    capacity = (IN_BLK + owners - 1) // owners
    offsets = jnp.cumsum(arrive_len) - arrive_len
    lane_index = jnp.arange(capacity, dtype=jnp.int32)[None, :]
    target_ids = jnp.arange(owners, dtype=jnp.int32)[:, None]
    slot_index = (target_ids - offsets[my_owner]) % owners + lane_index * owners
    packed = jnp.take(frames_in, jnp.minimum(slot_index, IN_BLK - 1).reshape(-1), axis=0)
    packed, proj_weight = lax.optimization_barrier((packed, proj_weight))
    arrived = lax.all_to_all(packed, "tm", split_axis=0, concat_axis=0, tiled=True)
    pieces = []
    for half in (0, 2):
        pieces += [proj_weight[half, :, :RANK], proj_weight[half + 1, :, :RANK]]
        pieces += [proj_weight[half, :, RANK:], proj_weight[half + 1, :, RANK:]]
    proj = jnp.concatenate(pieces, axis=1)
    spaces = lax.axis_size("space")
    order = (space_index - jnp.arange(spaces, dtype=jnp.int32)) % spaces

    def to_next(array, k):
        return lax.ppermute(array, "space", [(i, (i + k) % spaces) for i in range(spaces)])

    def gathered(array):
        shares = [array] + [to_next(array, k) for k in range(1, spaces)]
        return jnp.take(jnp.stack(shares), order, axis=0)

    proj = gathered(proj).reshape(spaces * part, 2 * HALF)
    wanted = jnp.arange(OWN_BLK, dtype=jnp.int32) * owners + my_owner
    sender = jnp.sum((offsets[None, :] <= wanted[:, None]).astype(jnp.int32), axis=1) - 1
    lane_of = (wanted - offsets[sender]) // owners
    owned = jnp.take(arrived, sender * capacity + lane_of, axis=0)
    full = lax.all_gather(owned, "space", axis=1, tiled=True).reshape(OWN_BLK, patches, width)

    def per_frame(*dims):
        return pl.BlockSpec((1,) + dims, lambda i: (i, 0, 0))

    def same_each(array):
        return pl.BlockSpec(array.shape, lambda i: (0,) * array.ndim)

    rests = (weight, in_weight, norm_gain[None, :], proj, pick)
    inner, stats, tiles, gate = pl.pallas_call(
        first_kernel,
        grid=(OWN_BLK,),
        out_shape=(
            jax.ShapeDtypeStruct((OWN_BLK, patches, part), BF16),
            jax.ShapeDtypeStruct((OWN_BLK, patches, HALF), BF16),
            jax.ShapeDtypeStruct((OWN_BLK, owners * slots, part + HALF), BF16),
            jax.ShapeDtypeStruct((OWN_BLK, owners * slots, part), BF16),
        ),
        in_specs=[per_frame(patches, width), same_each(weight)]
        + [pl.BlockSpec((1,) + in_weight.shape[1:], lambda i: (0, 0, 0))]
        + [same_each(a) for a in rests[2:]],
        out_specs=(
            per_frame(patches, part),
            per_frame(patches, HALF),
            per_frame(owners * slots, part + HALF),
            per_frame(owners * slots, part),
        ),
        compiler_params=pltpu.CompilerParams(vmem_limit_bytes=40 * 1024 * 1024),
        cost_estimate=pl.CostEstimate(
            flops=4_000_000_000, bytes_accessed=4_000_000, transcendentals=1_000_000
        ),
    )(full, *rests)

    def to_owner(array):
        moved = lax.all_to_all(array, "tm", split_axis=1, concat_axis=0, tiled=True)
        moved = moved.reshape(frames_total, ROWS, groups, array.shape[-1])
        return jnp.swapaxes(moved, 0, 1).reshape(ROWS, frames_total * groups, array.shape[-1])

    early = to_owner(tiles)
    late = call(
        spatial_kernel,
        jax.ShapeDtypeStruct((OWN_BLK, owners * slots, 2 * part), BF16),
        scan_scratch(patches, part),
        20_000_000_000,
        inner, stats, gate, pick, perm, inverse, spread, (dt_wide, 0), (bias, 0), (rate, 0),
        (skip[0] + skip[1])[None, :],
    )
    late = to_owner(late)

    clip_start = jnp.cumsum(clip_len) - clip_len
    row_frame = jnp.arange(frames_total, dtype=jnp.int32)
    row_frame = (row_frame % OWN_BLK) * owners + row_frame // OWN_BLK
    opens = jnp.any(row_frame[:, None] == clip_start[None, :], axis=1) | (row_frame == 0)
    closes = jnp.any(row_frame[:, None] == (clip_start + clip_len - 1)[None, :], axis=1)
    closes = closes | (row_frame == frames_total - 1)
    closed = jnp.stack([opens, closes], axis=1).astype(F32)
    closed = jnp.repeat(closed, groups, axis=0)
    rows = frames_total * groups
    temporal = call(
        functools.partial(temporal_kernel, frames_total, groups, part),
        jax.ShapeDtypeStruct((rows, lanes_of(part)), F32),
        scan_scratch(rows, part),
        20_000_000_000,
        early, closed, perm, spread, (dt_wide, 1), (bias, 1), (rate, 1), (skip[2] + skip[3])[None, :],
    )
    term = call(
        output_kernel,
        jax.ShapeDtypeStruct((ROWS, rows, width), BF16),
        [],
        2_000_000_000,
        temporal, late, perm, inverse, out_weight,
    )
    term = term.reshape(ROWS, owners, OWN_BLK, groups, width)
    term = jnp.transpose(term, (2, 1, 0, 3, 4)).reshape(frames_total, slots, width)[:, :per_owner]
    term = term.reshape(spaces, frames_total // spaces, per_owner, width)
    term = lax.all_to_all(term, "space", split_axis=0, concat_axis=0, tiled=True)
    mixed = jnp.sum(term.astype(F32), axis=0).astype(BF16)
    return jnp.swapaxes(mixed, 0, 1).reshape(per_owner, frames_total // spaces * width)


def solution(mesh):
    placed = (
        P(("groups", "tm"), "space"),
        P("groups"),
        P("groups"),
        P("groups", None),
        P(),
        P(),
        P(None, "space", None),
        P(None, None, "space"),
        P(None, "space"),
        P(None, "space", None),
        P(None, "space"),
        P("space", None),
    )
    return jax.shard_map(
        body, mesh=mesh, in_specs=placed, out_specs=P("tm", ("groups", "space")), check_vma=False
    )
```

```python
import functools

import jax
import jax.numpy as jnp
import numpy as np
from jax import lax
from jax.experimental import pallas as pl
from jax.experimental.pallas import tpu as pltpu
from jax.sharding import PartitionSpec as P

PATCHES = 196
OWN_BLK = 4
IN_BLK = 8
ROWS = 4
STATE = 16
RANK = 36
HALF = 2 * (RANK + 2 * STATE)
EPSILON = 1e-05
LOG2E = 1.4426950408889634
CLOSED = 1e4
F32 = jnp.float32
BF16 = jnp.bfloat16


def chunks_of(part):
    assert 0 < part % 128 <= 32
    return tuple((512 * i, 512) for i in range(part // 128)) + ((512 * (part // 128), 128),)


def lanes_of(part):
    return 512 * (part // 128) + 128


def constants():
    perm = np.zeros((512, 512), np.float32)
    for r in range(ROWS):
        for ch in range(128):
            perm[r * 128 + ch, (ch // 32) * 128 + r * 32 + ch % 32] = 1
    spread = np.zeros((ROWS * STATE, STATE * 128), np.float32)
    for r in range(ROWS):
        for s in range(STATE):
            spread[r * STATE + s, s * 128 + r * 32 : s * 128 + r * 32 + 32] = 1
    return perm, spread


def widening(part):
    widen = np.zeros((part, lanes_of(part)), np.float32)
    for ch in range(part):
        for r in range(ROWS):
            widen[ch, (ch // 32) * 128 + r * 32 + ch % 32] = 1
    return widen


PERM, SPREAD = constants()


def dot(a, b):
    return jnp.dot(a, b, preferred_element_type=F32)


def pack_rows(wide, tail, perm_ref, chunk, size):
    wide = wide if size == 512 else None
    if wide is not None:
        return dot(jnp.concatenate([wide(r, chunk) for r in range(ROWS)], axis=1), perm_ref[...])
    total = 0.0
    for r in range(ROWS):
        piece = tail(r)
        total = total + dot(piece, perm_ref[128 * r : 128 * r + piece.shape[1], 0:128])
    return total


def store_tiles(ref, k, start, block):
    rows = ref.shape[1]
    flat = ref.reshape(2, rows * STATE, 128)
    for t in range(block.shape[1] // 128):
        flat[k, pl.ds(start // 128 + t, rows, stride=STATE), :] = block[:, 128 * t : 128 * t + 128]


def load_sums(ref, start, size):
    rows, each = ref.shape[1], ref.shape[2]
    flat = ref.reshape(2, rows * each, 128)
    parts = []
    for t in range(start // 128, (start + size) // 128):
        terms = [flat[k, pl.ds(8 * t + s, rows, stride=each), :] for k in range(2) for s in range(8)]
        parts.append(sum(terms[1:], terms[0]))
    return jnp.concatenate(parts, axis=1)


def prepare(part, values, stats_ref, base, closed, weights, scratch):
    perm_ref, spread_ref, dt_ref, bias_ref = weights
    u_ref, d_ref, x_ref, b_ref, c_ref = scratch
    wide, tail = values
    stats = [stats_ref[r, :, base : base + HALF].astype(F32) for r in range(ROWS)]
    for k in range(2):
        low = jnp.concatenate([s[:, RANK * k : RANK * k + RANK] for s in stats], axis=1).astype(BF16)
        for chunk, (start, size) in enumerate(chunks_of(part)):
            cols = slice(start, start + size)
            if k == 0:
                u_ref[:, cols] = pack_rows(wide, tail, perm_ref, chunk, size)
            delta = dot(low, dt_ref[k, :, cols]) + bias_ref[k, :, cols]
            delta = jnp.maximum(delta, 0.0) + jnp.log1p(jnp.exp(-jnp.abs(delta)))
            store_tiles(x_ref, k, start, delta * u_ref[:, cols])
            if closed is not None:
                delta = jnp.where(closed[k] > 0.0, CLOSED, delta)
            store_tiles(d_ref, k, start, delta)
        for which, out_ref in ((0, b_ref), (1, c_ref)):
            at = 2 * RANK + STATE * (2 * k + which)
            picked = jnp.concatenate([s[:, at : at + STATE] for s in stats], axis=1).astype(BF16)
            for q in range(4):
                block = dot(picked, spread_ref[:, 512 * q : 512 * q + 512])
                store_tiles(out_ref, k, 512 * q, block)


def scan(k, steps, unroll, row_of, scratch, rate_ref, y_ref):
    u_ref, d_ref, x_ref, b_ref, c_ref = scratch
    tiles = u_ref.shape[1] // 128

    def step(i, state):
        row = row_of(i)
        b_now = b_ref[k, row]
        c_now = c_ref[k, row]
        after = []
        for t in range(tiles):
            cols = slice(128 * t, 128 * t + 128)
            d_now = jnp.broadcast_to(d_ref[k, row, t : t + 1, :], (STATE, 128))
            x_now = jnp.broadcast_to(x_ref[k, row, t : t + 1, :], (STATE, 128))
            h = jnp.exp2(d_now * rate_ref[k, :, cols]) * state[t] + x_now * b_now
            product = h * c_now
            y_ref[k, row, 8 * t : 8 * t + 8, :] = product[0:8] + product[8:16]
            after.append(h)
        return tuple(after)

    start = tuple(jnp.zeros((STATE, 128), F32) for _ in range(tiles))
    lax.fori_loop(0, steps, step, start, unroll=unroll)


def silu(v):
    return v * jax.nn.sigmoid(v)


def first_kernel(
    x_ref, w_ref, all_ref, gain_ref, proj_ref, pick_ref, inner_ref, stats_ref, tiles_ref, gate_ref
):
    x = x_ref[0].astype(F32)
    scale = lax.rsqrt(jnp.mean(x * x, axis=1, keepdims=True) + EPSILON)
    normed = (x * scale * gain_ref[...]).astype(BF16)
    part = inner_ref.shape[2]
    inner = silu(dot(normed, w_ref[0])).astype(BF16)
    gate = dot(normed, w_ref[1]).astype(BF16)
    inner_ref[0] = inner
    whole = silu(dot(normed, all_ref[0])).astype(BF16)
    stats = dot(whole, proj_ref[...]).astype(BF16)
    stats_ref[0] = stats[:, :HALF]
    pick = pick_ref[...]
    tiles_ref[0, :, :part] = dot(pick, inner).astype(BF16)
    tiles_ref[0, :, part:] = dot(pick, stats[:, HALF:]).astype(BF16)
    gate_ref[0] = dot(pick, gate).astype(BF16)


def spatial_kernel(
    inner_ref, stats_ref, gate_ref, pick_ref, perm_ref, inverse_ref, spread_ref, dt_ref, bias_ref, rate_ref,
    skip_ref, out_ref, u_ref, d_ref, x_ref, b_ref, c_ref, y_ref
):
    scratch = (u_ref, d_ref, x_ref, b_ref, c_ref)
    length, part = u_ref.shape[0], inner_ref.shape[2]
    cut = part // 128 * 128
    tail = part - cut
    values = (
        lambda r, c: inner_ref[r, :, 128 * c : 128 * c + 128],
        lambda r: inner_ref[r, :, cut:],
    )
    prepare(part, values, stats_ref, 0, None, (perm_ref, spread_ref, dt_ref, bias_ref), scratch)
    scan(0, length, 7, lambda i: i, scratch, rate_ref, y_ref)
    scan(1, length, 7, lambda i: length - 1 - i, scratch, rate_ref, y_ref)
    pick = pick_ref[...]
    for start, size in chunks_of(part):
        cols = slice(start, start + size)
        total = load_sums(y_ref, start, size)
        total = total + skip_ref[:, cols] * u_ref[:, cols]
        total = dot(pick, total.astype(BF16)).astype(BF16)
        if size == 512:
            back = dot(total, inverse_ref[...]).astype(BF16)
            for r in range(ROWS):
                at = start // 4
                out_ref[r, :, at : at + 128] = back[:, 128 * r : 128 * r + 128]
        else:
            for r in range(ROWS):
                back = dot(total, inverse_ref[0:128, 128 * r : 128 * r + tail])
                out_ref[r, :, 2 * cut : 2 * cut + tail] = back.astype(BF16)
    for r in range(ROWS):
        out_ref[r, :, cut : 2 * cut] = gate_ref[r, :, :cut]
        out_ref[r, :, 2 * cut + tail :] = gate_ref[r, :, cut:]


def temporal_kernel(
    frames, groups, part, moved_ref, closed_ref, perm_ref, spread_ref, dt_ref, bias_ref, rate_ref,
    skip_ref, out_ref, u_ref, d_ref, x_ref, b_ref, c_ref, y_ref
):
    scratch = (u_ref, d_ref, x_ref, b_ref, c_ref)
    owners = frames // OWN_BLK
    cut = part // 128 * 128
    values = (
        lambda r, c: moved_ref[r, :, 128 * c : 128 * c + 128],
        lambda r: moved_ref[r, :, cut:part],
    )
    closed = (closed_ref[:, 0:1], closed_ref[:, 1:2])
    prepare(part, values, moved_ref, part, closed, (perm_ref, spread_ref, dt_ref, bias_ref), scratch)

    def row_at(i, backward):
        group, frame = i // frames, i % frames
        if backward:
            frame = frames - 1 - frame
        return ((frame % owners) * OWN_BLK + frame // owners) * groups + group

    steps = frames * groups
    scan(0, steps, 8, lambda i: row_at(i, False), scratch, rate_ref, y_ref)
    scan(1, steps, 8, lambda i: row_at(i, True), scratch, rate_ref, y_ref)
    for start, size in chunks_of(part):
        cols = slice(start, start + size)
        total = load_sums(y_ref, start, size)
        out_ref[:, cols] = total + skip_ref[:, cols] * u_ref[:, cols]


def output_kernel(temporal_ref, moved_ref, perm_ref, inverse_ref, w_ref, out_ref):
    part = w_ref.shape[0]
    cut = part // 128 * 128
    tail = part - cut
    spatial = (
        lambda r, c: moved_ref[r, :, 128 * c : 128 * c + 128],
        lambda r: moved_ref[r, :, 2 * cut : 2 * cut + tail],
    )
    gate = (
        lambda r, c: moved_ref[r, :, cut + 128 * c : cut + 128 * c + 128],
        lambda r: moved_ref[r, :, 2 * cut + tail :],
    )
    backs = []
    for chunk, (start, size) in enumerate(chunks_of(part)):
        total = temporal_ref[:, start : start + size] + pack_rows(*spatial, perm_ref, chunk, size)
        total = (total * silu(pack_rows(*gate, perm_ref, chunk, size))).astype(BF16)
        if size == 512:
            total = dot(total, inverse_ref[...]).astype(BF16)
        backs.append(total)
    for r in range(ROWS):
        lanes = slice(128 * r, 128 * r + 128)
        last = dot(backs[-1], inverse_ref[0:128, 128 * r : 128 * r + tail]).astype(BF16)
        term = dot(last, w_ref[cut:, :])
        for c in range(cut // 128):
            term = term + dot(backs[c][:, lanes], w_ref[128 * c : 128 * c + 128, :])
        out_ref[r] = term.astype(BF16)


def scan_scratch(rows, part):
    lanes = lanes_of(part)
    inputs = [pltpu.VMEM((2, rows, STATE, 128), F32)] * 4
    return [pltpu.VMEM((rows, lanes), F32)] + inputs + [pltpu.VMEM((2, rows, lanes // 16, 128), F32)]


def call(kernel, out_shape, scratch, flops, *operands):
    specs, arrays = [], []
    for operand in operands:
        array, half = operand if isinstance(operand, tuple) else (operand, None)
        arrays.append(array)
        if half is None:
            specs.append(pl.BlockSpec(memory_space=pltpu.VMEM))
        else:
            specs.append(pl.BlockSpec((2,) + array.shape[1:], functools.partial(lambda h, i: (h, 0, 0), half)))
    return pl.pallas_call(
        kernel,
        grid=(1,),
        out_shape=out_shape,
        in_specs=specs,
        out_specs=pl.BlockSpec(memory_space=pltpu.VMEM),
        scratch_shapes=scratch,
        compiler_params=pltpu.CompilerParams(vmem_limit_bytes=56 * 1024 * 1024),
        cost_estimate=pl.CostEstimate(flops=flops, bytes_accessed=8_000_000, transcendentals=7_000_000),
    )(*arrays)


def body(
    frames_in, arrive_len, clip_len, tile_pick, norm_gain, in_weight, proj_weight, dt_weight, dt_bias,
    decay_rate, skip_gain, out_weight
):
    owners = lax.axis_size("tm")
    my_owner = lax.axis_index("tm")
    space_index = lax.axis_index("space")
    patches = PATCHES
    width = in_weight.shape[1]
    part = out_weight.shape[0]
    frames_total = owners * OWN_BLK
    per_owner = tile_pick.shape[1] // owners
    groups = -(-per_owner // ROWS)
    slots = ROWS * groups

    weight = lax.dynamic_slice_in_dim(in_weight, space_index * part, part, 2)
    widen = jnp.asarray(widening(part))
    exact = functools.partial(
        jnp.einsum, precision=lax.Precision.HIGHEST, preferred_element_type=F32
    )
    rate = exact("kcs,cn->ksn", decay_rate, widen) * -LOG2E
    bias = exact("kc,cn->kn", dt_bias, widen)[:, None, :]
    skip = exact("kc,cn->kn", skip_gain, widen)
    dt_wide = jnp.einsum(
        "kic,cn->kin", dt_weight, widen.astype(BF16), preferred_element_type=F32
    ).astype(BF16)
    lane_row = (jnp.arange(lanes_of(part), dtype=jnp.int32) % 128) // 32
    same = (lane_row[None, :] == jnp.arange(ROWS, dtype=jnp.int32)[:, None])[None, :, None, :]
    dt_wide = jnp.where(same, dt_wide[:, None], jnp.zeros((), BF16)).reshape(4, ROWS * RANK, lanes_of(part))
    pick = tile_pick.astype(BF16).T.reshape(owners, per_owner, patches)
    pick = jnp.pad(pick, ((0, 0), (0, slots - per_owner), (0, 0))).reshape(owners * slots, patches)
    perm, inverse = jnp.asarray(PERM, BF16), jnp.asarray(PERM.T, BF16)
    spread = jnp.asarray(SPREAD, BF16)

    capacity = (IN_BLK + owners - 1) // owners
    offsets = jnp.cumsum(arrive_len) - arrive_len
    lane_index = jnp.arange(capacity, dtype=jnp.int32)[None, :]
    target_ids = jnp.arange(owners, dtype=jnp.int32)[:, None]
    slot_index = (target_ids - offsets[my_owner]) % owners + lane_index * owners
    packed = jnp.take(frames_in, jnp.minimum(slot_index, IN_BLK - 1).reshape(-1), axis=0)
    packed, proj_weight = lax.optimization_barrier((packed, proj_weight))
    arrived = lax.all_to_all(packed, "tm", split_axis=0, concat_axis=0, tiled=True)
    pieces = []
    for half in (0, 2):
        pieces += [proj_weight[half, :, :RANK], proj_weight[half + 1, :, :RANK]]
        pieces += [proj_weight[half, :, RANK:], proj_weight[half + 1, :, RANK:]]
    proj = jnp.concatenate(pieces, axis=1)
    spaces = lax.axis_size("space")
    order = (space_index - jnp.arange(spaces, dtype=jnp.int32)) % spaces

    def to_next(array, k):
        return lax.ppermute(array, "space", [(i, (i + k) % spaces) for i in range(spaces)])

    def gathered(array):
        shares = [array] + [to_next(array, k) for k in range(1, spaces)]
        return jnp.take(jnp.stack(shares), order, axis=0)

    proj = gathered(proj).reshape(spaces * part, 2 * HALF)
    wanted = jnp.arange(OWN_BLK, dtype=jnp.int32) * owners + my_owner
    sender = jnp.sum((offsets[None, :] <= wanted[:, None]).astype(jnp.int32), axis=1) - 1
    lane_of = (wanted - offsets[sender]) // owners
    owned = jnp.take(arrived, sender * capacity + lane_of, axis=0)
    full = lax.all_gather(owned, "space", axis=1, tiled=True).reshape(OWN_BLK, patches, width)

    def per_frame(*dims):
        return pl.BlockSpec((1,) + dims, lambda i: (i, 0, 0))

    def same_each(array):
        return pl.BlockSpec(array.shape, lambda i: (0,) * array.ndim)

    rests = (weight, in_weight, norm_gain[None, :], proj, pick)
    inner, stats, tiles, gate = pl.pallas_call(
        first_kernel,
        grid=(OWN_BLK,),
        out_shape=(
            jax.ShapeDtypeStruct((OWN_BLK, patches, part), BF16),
            jax.ShapeDtypeStruct((OWN_BLK, patches, HALF), BF16),
            jax.ShapeDtypeStruct((OWN_BLK, owners * slots, part + HALF), BF16),
            jax.ShapeDtypeStruct((OWN_BLK, owners * slots, part), BF16),
        ),
        in_specs=[per_frame(patches, width), same_each(weight)]
        + [pl.BlockSpec((1,) + in_weight.shape[1:], lambda i: (0, 0, 0))]
        + [same_each(a) for a in rests[2:]],
        out_specs=(
            per_frame(patches, part),
            per_frame(patches, HALF),
            per_frame(owners * slots, part + HALF),
            per_frame(owners * slots, part),
        ),
        compiler_params=pltpu.CompilerParams(vmem_limit_bytes=40 * 1024 * 1024),
        cost_estimate=pl.CostEstimate(
            flops=4_000_000_000, bytes_accessed=4_000_000, transcendentals=1_000_000
        ),
    )(full, *rests)

    def to_owner(array):
        moved = lax.all_to_all(array, "tm", split_axis=1, concat_axis=0, tiled=True)
        moved = moved.reshape(frames_total, ROWS, groups, array.shape[-1])
        return jnp.swapaxes(moved, 0, 1).reshape(ROWS, frames_total * groups, array.shape[-1])

    early = to_owner(tiles)
    late = call(
        spatial_kernel,
        jax.ShapeDtypeStruct((OWN_BLK, owners * slots, 2 * part), BF16),
        scan_scratch(patches, part),
        20_000_000_000,
        inner, stats, gate, pick, perm, inverse, spread, (dt_wide, 0), (bias, 0), (rate, 0),
        (skip[0] + skip[1])[None, :],
    )
    late = to_owner(late)

    clip_start = jnp.cumsum(clip_len) - clip_len
    row_frame = jnp.arange(frames_total, dtype=jnp.int32)
    row_frame = (row_frame % OWN_BLK) * owners + row_frame // OWN_BLK
    opens = jnp.any(row_frame[:, None] == clip_start[None, :], axis=1) | (row_frame == 0)
    closes = jnp.any(row_frame[:, None] == (clip_start + clip_len - 1)[None, :], axis=1)
    closes = closes | (row_frame == frames_total - 1)
    closed = jnp.stack([opens, closes], axis=1).astype(F32)
    closed = jnp.repeat(closed, groups, axis=0)
    rows = frames_total * groups
    temporal = call(
        functools.partial(temporal_kernel, frames_total, groups, part),
        jax.ShapeDtypeStruct((rows, lanes_of(part)), F32),
        scan_scratch(rows, part),
        20_000_000_000,
        early, closed, perm, spread, (dt_wide, 1), (bias, 1), (rate, 1), (skip[2] + skip[3])[None, :],
    )
    term = call(
        output_kernel,
        jax.ShapeDtypeStruct((ROWS, rows, width), BF16),
        [],
        2_000_000_000,
        temporal, late, perm, inverse, out_weight,
    )
    term = term.reshape(ROWS, owners, OWN_BLK, groups, width)
    term = jnp.transpose(term, (2, 1, 0, 3, 4)).reshape(frames_total, slots, width)[:, :per_owner]
    term = term.reshape(spaces, frames_total // spaces, per_owner, width)
    term = lax.all_to_all(term, "space", split_axis=0, concat_axis=0, tiled=True)
    mixed = jnp.sum(term.astype(F32), axis=0).astype(BF16)
    return jnp.swapaxes(mixed, 0, 1).reshape(per_owner, frames_total // spaces * width)


def solution(mesh):
    placed = (
        P(("groups", "tm"), "space"),
        P("groups"),
        P("groups"),
        P("groups", None),
        P(),
        P(),
        P(None, "space", None),
        P(None, None, "space"),
        P(None, "space"),
        P(None, "space", None),
        P(None, "space"),
        P("space", None),
    )
    return jax.shard_map(
        body, mesh=mesh, in_specs=placed, out_specs=P("tm", ("groups", "space")), check_vma=False
    )
```
